128 devices in a mesh: segment: 2 (over z_hi), dp: 16 (over x, y), mp: 4 (over z_lo, core).
Axes of the slice: x: 4, y: 4, z: 4 (z_hi: 2, z_lo: 2; z = z_hi * 2 + z_lo), core: 2. Of those that a mesh axis runs over, the one named last changes fastest.
Arguments:
- token_ids: int32 [2, 256], replicated, may hold values from 0 to 32767
- table: bfloat16 [32768, 8192], P('dp', 'mp'), may hold values from -6 to 6
- w_up: bfloat16 [2, 8192, 32768], P('segment', 'mp', 'dp'), may hold values from -0.0625 to 0.0625
- w_down: bfloat16 [2, 32768, 8192], P('segment', 'dp', 'mp'), may hold values from -0.03125 to 0.03125
- cotangent: bfloat16 [2, 256, 8192], P(None, 'dp', 'mp'), may hold values from -6 to 6
Outputs:
- acts: bfloat16 [2, 2, 256, 8192], P('segment', None, 'dp', 'mp')
- grads: bfloat16 [2, 2, 256, 8192], P('segment', None, 'dp', 'mp')
The draws below stay inside these ranges and needn't reach their ends.
All inputs are finite; a program needn't handle non-finite values.
Results may differ from the reference program's by a relative error of at most 0.018.
Values may be sent and summed in bfloat16 or wider, within the bound.
No kernel may reach another device: no remote copies, remote signals or barrier semaphores. Data moves between devices by JAX's collectives and lax.ppermute only.
A program may use at most 128 MiB of HBM per device.

```python
import math
import jax
import jax.numpy as jnp
import numpy as np
from jax import lax

D = 8192
FF = 32768
VOCAB = 32768
MICRO = 2
TOK_MB = 256
SEGMENTS = 2


def touch_ends(array, stream_key, smallest, top_value):
    dims = array.shape
    place = [jax.random.randint(jax.random.fold_in(stream_key, axis), (), 0, dims[axis]) for axis in range(len(dims))]
    array = array.at[tuple(place)].set(smallest)
    longest = dims.index(max(dims))
    place[longest] = (place[longest] + 1) % dims[longest]
    return array.at[tuple(place)].set(top_value)


def steps_of(key, shape, split, least, high):
    factor_of, own = 1.0, jax.random.fold_in(key, 6)
    for dim, shards_of in split:
        heights = jnp.exp(jax.random.uniform(jax.random.fold_in(own, dim), (shards_of,), jnp.float32, least / len(split), high / len(split)))
        factor_of = factor_of * jnp.repeat(heights, shape[dim] // shards_of).reshape([-1 if axis == dim else 1 for axis in range(len(shape))])
    return factor_of


def cumulative_ranks(amount, slope):
    loads = [(1 << 20) // math.isqrt(grade ** slope) + 1 for grade in range(1, amount + 1)]
    spread = 1 + sum(loads) // (1 << 30)
    return np.cumsum(np.array([max(1, weight // spread) for weight in loads]))


def ranked(rng, extent, number_of, slope):
    listing = cumulative_ranks(number_of, slope)
    pick = jax.random.randint(jax.random.fold_in(rng, 1), extent, 0, int(listing[number_of - 1]))
    standing = jnp.searchsorted(jnp.asarray(listing, jnp.int32), pick, side="right")
    return jax.random.permutation(jax.random.fold_in(rng, 2), number_of)[standing].astype(jnp.int32)


def centred(rng, shape, scale, most, shards=(), dtype=jnp.bfloat16):
    values = scale * jax.random.normal(rng, shape, jnp.float32)
    if shards:
        values = values * steps_of(rng, shape, shards, -0.22, 0.18)
    return jnp.clip(values, -most, most).astype(dtype)


def setup_inputs(seed: int = 0) -> dict:
    key_of = jax.random.split(jax.random.key(seed), 6)
    token_ids = touch_ends(ranked(key_of[0], (MICRO, TOK_MB), VOCAB, 2), jax.random.fold_in(key_of[0], 3), 0, VOCAB - 1).astype(jnp.int32)
    table = centred(key_of[1], (VOCAB, D), 1.0, 6.0, ((0, 16), (1, 4)))
    w_up = centred(key_of[2], (SEGMENTS, D, FF), D ** -0.5, 0.0625, ((0, 2), (1, 4), (2, 16)))
    w_down = centred(key_of[3], (SEGMENTS, FF, D), FF ** -0.5, 0.03125, ((0, 2), (1, 16), (2, 4)))
    cotangent = centred(key_of[4], (MICRO, TOK_MB, D), 1.0, 6.0, ((1, 16), (2, 4)))
    return dict(token_ids=token_ids, table=table, w_up=w_up, w_down=w_down, cotangent=cotangent)


root_coef = 0.7978845608028654


def gelu_value(value):
    return 0.5 * value * (1.0 + jnp.tanh(root_coef * (value + 0.044715 * value * value * value)))


def gelu_slope(value):
    inner = jnp.tanh(root_coef * (value + 0.044715 * value * value * value))
    return 0.5 * (1.0 + inner) + 0.5 * value * (1.0 - inner * inner) * root_coef * (1.0 + 0.134145 * value * value)


def section_forward(inputs, up_matrix, down_matrix):
    pre_act = jnp.dot(inputs, up_matrix, preferred_element_type=jnp.float32)
    hidden = gelu_value(pre_act).astype(jnp.bfloat16)
    mixed = jnp.dot(hidden, down_matrix, preferred_element_type=jnp.float32)
    return (inputs.astype(jnp.float32) + mixed).astype(jnp.bfloat16), pre_act


def section_backward(upstream, pre_act, up_matrix, down_matrix):
    back_hidden = lax.dot_general(upstream, down_matrix, (((1,), (1,)), ((), ())), preferred_element_type=jnp.float32)
    back_pre = (gelu_slope(pre_act) * back_hidden).astype(jnp.bfloat16)
    mixed = lax.dot_general(back_pre, up_matrix, (((1,), (1,)), ((), ())), preferred_element_type=jnp.float32)
    return (upstream.astype(jnp.float32) + mixed).astype(jnp.bfloat16)


def reference(token_ids, table, w_up, w_down, cotangent):
    first_outs, second_outs, first_grads, second_grads = [], [], [], []
    for micro_pos in range(MICRO):
        embedded = jnp.take(table, token_ids[micro_pos], axis=0)
        first_out, first_pre = section_forward(embedded, w_up[0], w_down[0])
        second_out, second_pre = section_forward(first_out, w_up[1], w_down[1])
        second_grad = section_backward(cotangent[micro_pos], second_pre, w_up[1], w_down[1])
        first_grad = section_backward(second_grad, first_pre, w_up[0], w_down[0])
        first_outs.append(first_out)
        second_outs.append(second_out)
        first_grads.append(first_grad)
        second_grads.append(second_grad)
    acts = jnp.stack([jnp.stack(first_outs), jnp.stack(second_outs)])
    grads = jnp.stack([jnp.stack(first_grads), jnp.stack(second_grads)])
    return acts, grads
```

```python
import jax
import jax.numpy as jnp
from jax import lax
from jax.sharding import PartitionSpec as P

root_coef = 0.7978845608028654
chunk_count = 4


def gelu_value(value):
    return 0.5 * value * (1.0 + jnp.tanh(root_coef * (value + 0.044715 * value * value * value)))


def gelu_slope(value):
    inner = jnp.tanh(root_coef * (value + 0.044715 * value * value * value))
    return 0.5 * (1.0 + inner) + 0.5 * value * (1.0 - inner * inner) * root_coef * (
        1.0 + 0.134145 * value * value
    )


def swap(value, bit):
    return lax.ppermute(value, "mp", [(i, i ^ bit) for i in range(4)])


def exchange(blocks):
    return lax.all_to_all(blocks, "dp", 0, 0)


def spread(own):
    return jnp.broadcast_to(own[None], (lax.axis_size("dp"),) + own.shape)


def collect(blocks):
    return jnp.sum(blocks.astype(jnp.float32), axis=0)


def product(rows, weight, dim):
    return lax.dot_general(
        rows, weight, (((1,), (dim,)), ((), ())), preferred_element_type=jnp.float32
    )


def mp_sum(partial_sum, low_core):
    half = partial_sum.shape[0] // 2
    low, high = partial_sum[:half], partial_sum[half:]
    kept = jnp.where(low_core, low, high)
    sent = jnp.where(low_core, high, low).astype(jnp.bfloat16)
    chip = kept + swap(sent, 1).astype(jnp.float32)
    return chip + swap(chip.astype(jnp.bfloat16), 2).astype(jnp.float32)


def both_halves(mine, low_core):
    other = swap(mine, 1)
    return jnp.concatenate(
        [jnp.where(low_core, mine, other), jnp.where(low_core, other, mine)], axis=0
    )


def on_device(token_ids, table, w_up, w_down, cotangent):
    micro, tok, feat = cotangent.shape
    dp = lax.axis_size("dp")
    up = w_up[0]
    down = w_down[0]
    is_first = lax.axis_index("segment") == 0
    low_core = lax.axis_index("mp") % 2 == 0
    rows = micro * tok
    own_cot = cotangent.reshape(rows, feat)

    table_rows = table.shape[0]
    mine = lax.dynamic_index_in_dim(token_ids, lax.axis_index("segment"), 0, keepdims=False)
    picked = mine - lax.axis_index("dp") * table_rows
    inside = (picked >= 0) & (picked < table_rows)
    fetched = jnp.take(table, jnp.clip(picked, 0, table_rows - 1), axis=0)
    fetched = jnp.where(inside[:, None], fetched, jnp.zeros_like(fetched))
    found = collect(exchange(fetched.reshape(dp, tok, feat))).astype(jnp.bfloat16)
    other = lax.ppermute(found, "segment", [(0, 1), (1, 0)])
    embedded = jnp.concatenate(
        [jnp.where(is_first, found, other), jnp.where(is_first, other, found)], axis=0
    )

    def chunks(whole):
        step = whole.shape[0] // chunk_count
        return [whole[i * step : (i + 1) * step] for i in range(chunk_count)]

    def gathered(own):
        return exchange(spread(own)).reshape(dp * rows, feat)

    def first_product(whole, weight, dim):
        return [mp_sum(product(part, weight, dim), low_core) for part in chunks(whole)]

    def second_product(parts, weight, dim):
        return jnp.concatenate(
            [
                product(both_halves(part, low_core), weight, dim).astype(jnp.bfloat16)
                for part in parts
            ],
            axis=0,
        ).reshape(dp, rows, feat)

    entering = gathered(jnp.where(is_first, embedded, own_cot))
    first = [
        mp_sum(
            lax.cond(
                is_first,
                lambda part: product(part, up, 0),
                lambda part: product(part, down, 1),
                part,
            ),
            low_core,
        )
        for part in chunks(entering)
    ]
    hidden = [gelu_value(part).astype(jnp.bfloat16) for part in first]
    act0 = (
        embedded.astype(jnp.float32) + collect(exchange(second_product(hidden, down, 0)))
    ).astype(jnp.bfloat16)
    passed = lax.ppermute(act0, "segment", [(0, 1), (1, 0)])

    pre = first_product(gathered(passed), up, 0)
    back_pre = [
        (gelu_slope(part) * back).astype(jnp.bfloat16) for part, back in zip(pre, first)
    ]
    grad1 = (
        own_cot.astype(jnp.float32) + collect(exchange(second_product(back_pre, up, 1)))
    ).astype(jnp.bfloat16)
    returned = lax.ppermute(grad1, "segment", [(0, 1), (1, 0)])
    mixed1 = second_product([gelu_value(part).astype(jnp.bfloat16) for part in pre], down, 0)

    slot = exchange(jnp.where(is_first, spread(returned), mixed1))
    act1 = (passed.astype(jnp.float32) + collect(slot)).astype(jnp.bfloat16)
    back = first_product(slot.reshape(dp * rows, feat), down, 1)
    back_pre0 = [
        (gelu_slope(part) * grad).astype(jnp.bfloat16) for part, grad in zip(first, back)
    ]
    grad0 = (
        returned.astype(jnp.float32) + collect(exchange(second_product(back_pre0, up, 1)))
    ).astype(jnp.bfloat16)

    acts = jnp.where(is_first, act0, act1).reshape(1, micro, tok, feat)
    grads = jnp.where(is_first, grad0, grad1).reshape(1, micro, tok, feat)
    return (acts, grads)


def solution(mesh):
    return jax.shard_map(
        on_device,
        mesh=mesh,
        in_specs=(
            P(),
            P("dp", "mp"),
            P("segment", "mp", "dp"),
            P("segment", "dp", "mp"),
            P(None, "dp", "mp"),
        ),
        out_specs=(P("segment", None, "dp", "mp"), P("segment", None, "dp", "mp")),
        check_vma=False,
    )
```

```python
import functools

import jax
import jax.numpy as jnp
from jax import lax
from jax.experimental import pallas as pl
from jax.experimental.pallas import tpu as pltpu
from jax.sharding import PartitionSpec as P

root_coef = 0.7978845608028654
bf16, f32 = jnp.bfloat16, jnp.float32
tile = 512
cost = pl.CostEstimate(flops=200_000_000, bytes_accessed=1_000_000, transcendentals=0)
params = pltpu.CompilerParams(vmem_limit_bytes=24 * 1024 * 1024)


def gelu_value(value):
    return 0.5 * value * (1.0 + jnp.tanh(root_coef * (value + 0.044715 * value * value * value)))


def gelu_slope(value):
    inner = jnp.tanh(root_coef * (value + 0.044715 * value * value * value))
    return 0.5 * (1.0 + inner) + 0.5 * value * (1.0 - inner * inner) * root_coef * (
        1.0 + 0.134145 * value * value
    )


def swap(value, bit):
    return lax.ppermute(value, "mp", [(i, i ^ bit) for i in range(4)])


def across(value):
    return lax.ppermute(value, "segment", [(0, 1), (1, 0)])


def exchange(blocks):
    return lax.all_to_all(blocks, "dp", 0, 0)


def spread(own):
    return jnp.broadcast_to(own[None], (lax.axis_size("dp"),) + own.shape)


def collect(blocks):
    return jnp.sum(blocks.astype(f32), axis=0)


def plus(own, blocks):
    return (own.astype(f32) + collect(blocks)).astype(bf16)


def multiply(rows, weight, dim):
    return lax.dot_general(
        rows, weight, (((1,), (dim,)), ((), ())), preferred_element_type=f32
    )


def start_weight(weight, dim, held, arrived):
    copies = []
    for index in range(held.shape[0]):
        columns = pl.ds(index * tile, tile)
        source = weight.at[:, columns] if dim == 0 else weight.at[columns, :]
        copies.append(pltpu.make_async_copy(source, held.at[index], arrived.at[index]))
        copies[-1].start()
    return copies


def split_tiles(rows, copies, held, dim, low, staged_kept, staged_sent, kept, sent, left):
    half = kept.shape[0]
    pending = []
    for index, copy in enumerate(copies):
        copy.wait()
        total = multiply(rows[...], held[index], dim)
        staged_kept[index] = jnp.where(low, total[:half], total[half:])
        staged_sent[index] = jnp.where(low, total[half:], total[:half]).astype(bf16)
        columns = pl.ds(index * tile, tile)
        pending += [
            pltpu.make_async_copy(staged_sent.at[index], sent.at[:, columns], left.at[2 * index]),
            pltpu.make_async_copy(
                staged_kept.at[index], kept.at[:, columns], left.at[2 * index + 1]
            ),
        ]
        pending[-2].start()
        pending[-1].start()
    for copy in pending:
        copy.wait()


def split_kernel(dims, place, rows_in, *refs):
    weights, refs = refs[: len(dims)], refs[len(dims) :]
    kept, sent, rows, staged_kept, staged_sent, arrived, left = refs[:7]
    helds = refs[7:]
    rows_copy = pltpu.make_async_copy(rows_in, rows, arrived.at[arrived.shape[0] - 1])
    rows_copy.start()
    low = place[0] == 0

    def run(weight, dim, held):
        copies = start_weight(weight, dim, held, arrived)
        rows_copy.wait()
        split_tiles(rows, copies, held, dim, low, staged_kept, staged_sent, kept, sent, left)

    if len(dims) == 1:
        run(weights[0], dims[0], helds[0])
    else:
        for section in range(2):
            pl.when(place[1] == section)(
                functools.partial(run, weights[section], dims[section], helds[section])
            )


def held_shape(weight, dim):
    depth, count = weight.shape[dim], weight.shape[1 - dim]
    return (count // tile, depth, tile) if dim == 0 else (count // tile, tile, depth)


def split_product(rows, weights, dims, place):
    count = weights[0].shape[1 - dims[0]]
    tiles = count // tile
    half = rows.shape[0] // 2
    anywhere = pl.BlockSpec(memory_space=pl.ANY)
    return pl.pallas_call(
        functools.partial(split_kernel, dims),
        in_specs=[pl.BlockSpec(memory_space=pltpu.SMEM)] + [anywhere] * (1 + len(weights)),
        out_specs=[anywhere, anywhere],
        out_shape=[
            jax.ShapeDtypeStruct((half, count), f32),
            jax.ShapeDtypeStruct((half, count), bf16),
        ],
        scratch_shapes=[
            pltpu.VMEM(rows.shape, bf16),
            pltpu.VMEM((tiles, half, tile), f32),
            pltpu.VMEM((tiles, half, tile), bf16),
            pltpu.SemaphoreType.DMA((tiles + 1,)),
            pltpu.SemaphoreType.DMA((2 * tiles,)),
        ]
        + [pltpu.VMEM(held_shape(w, d), bf16) for w, d in zip(weights, dims)],
        compiler_params=params,
        cost_estimate=cost,
    )(place, rows, *weights)


def join_kernel(dim, place, mine, other, weight, out, rows, staged, arrived, left, held):
    half = mine.shape[0]
    tiles = held.shape[0]
    parts = [
        pltpu.make_async_copy(
            part,
            rows.at[pl.ds(pl.multiple_of(position * half, half), half)],
            arrived.at[tiles + index],
        )
        for index, (part, position) in enumerate(((mine, place[0]), (other, 1 - place[0])))
    ]
    for copy in parts:
        copy.start()
    copies = start_weight(weight, dim, held, arrived)
    for copy in parts:
        copy.wait()
    pending = []
    for index, copy in enumerate(copies):
        copy.wait()
        staged[index] = multiply(rows[...], held[index], dim).astype(bf16)
        pending.append(
            pltpu.make_async_copy(
                staged.at[index], out.at[:, pl.ds(index * tile, tile)], left.at[index]
            )
        )
        pending[-1].start()
    for copy in pending:
        copy.wait()


def join_product(mine, other, weight, dim, place):
    count = weight.shape[1 - dim]
    tiles = count // tile
    half, depth = mine.shape
    anywhere = pl.BlockSpec(memory_space=pl.ANY)
    return pl.pallas_call(
        functools.partial(join_kernel, dim),
        in_specs=[pl.BlockSpec(memory_space=pltpu.SMEM)] + [anywhere] * 3,
        out_specs=anywhere,
        out_shape=jax.ShapeDtypeStruct((2 * half, count), bf16),
        scratch_shapes=[
            pltpu.VMEM((2 * half, depth), bf16),
            pltpu.VMEM((tiles, 2 * half, tile), bf16),
            pltpu.SemaphoreType.DMA((tiles + 2,)),
            pltpu.SemaphoreType.DMA((tiles,)),
            pltpu.VMEM(held_shape(weight, dim), bf16),
        ],
        compiler_params=params,
        cost_estimate=cost,
    )(place, mine, other, weight)


def lookup_kernel(wanted, table, out, chosen):
    @pl.when(pl.program_id(0) == 0)
    def _():
        row = lax.broadcasted_iota(jnp.int32, chosen.shape, 1)
        chosen[...] = jnp.where(row == wanted[...], 1.0, 0.0).astype(bf16)

    out[...] = multiply(chosen[...], table[...], 0).astype(bf16)


def lookup(wanted, table):
    count = wanted.shape[0]
    rows, feat = table.shape
    return pl.pallas_call(
        lookup_kernel,
        grid=(feat // tile,),
        in_specs=[
            pl.BlockSpec(wanted.shape, lambda i: (0, 0)),
            pl.BlockSpec((rows, tile), lambda i: (0, i)),
        ],
        out_specs=pl.BlockSpec((count, tile), lambda i: (0, i)),
        scratch_shapes=[pltpu.VMEM((count, rows), bf16)],
        out_shape=jax.ShapeDtypeStruct((count, feat), bf16),
        compiler_params=params,
        cost_estimate=cost,
    )(wanted, table)


def tie(*values):
    return lax.optimization_barrier(values)


def on_device(token_ids, table, w_up, w_down, cotangent):
    micro, tok, feat = cotangent.shape
    dp = lax.axis_size("dp")
    up = w_up[0]
    down = w_down[0]
    is_first = lax.axis_index("segment") == 0
    place = jnp.stack([lax.axis_index("mp") % 2, lax.axis_index("segment")]).astype(jnp.int32)

    def whole(slot):
        return slot.reshape(dp * tok, feat)

    def blocks(rows):
        return rows.reshape(dp, tok, feat)

    def either(left, right):
        return jnp.where(is_first, left, right)

    def chip_sum(kept, sent):
        chip = kept + swap(sent, 1).astype(f32)
        return chip, swap(chip.astype(bf16), 2)

    def finish(chip, came):
        return chip + came.astype(f32)

    def active(summed):
        return gelu_value(summed).astype(bf16)

    def slope(saved, summed):
        return (gelu_slope(saved) * summed).astype(bf16)

    mine = lax.dynamic_index_in_dim(token_ids, lax.axis_index("segment"), 0, keepdims=False)
    wanted = mine - lax.axis_index("dp") * table.shape[0]
    slot_1 = exchange(blocks(lookup(wanted[:, None], table)))
    found = collect(slot_1).astype(bf16)
    other = across(found)
    slot_2 = exchange(spread(either(found, cotangent[1])))
    send_3 = spread(either(other, cotangent[0]))
    emb_a, emb_b = either(found, other), either(other, found)
    slot_2, send_3 = tie(slot_2, send_3)

    kept_a, sent_a = split_product(whole(slot_2), (up, down), (0, 1), place)
    send_3, kept_a, sent_a = tie(send_3, kept_a, sent_a)
    slot_3 = exchange(send_3)
    chip_a, came_a = chip_sum(kept_a, sent_a)
    slot_3, chip_a = tie(slot_3, chip_a)
    kept_b, sent_b = split_product(whole(slot_3), (up, down), (0, 1), place)
    came_a, kept_b, sent_b = tie(came_a, kept_b, sent_b)
    first_a = finish(chip_a, came_a)
    hid_a = active(first_a)
    far_a = swap(hid_a, 1)
    chip_b, came_b = chip_sum(kept_b, sent_b)
    far_a, chip_b = tie(far_a, chip_b)
    mix_a = join_product(hid_a, far_a, down, 0, place)
    came_b, mix_a = tie(came_b, mix_a)
    slot_4 = exchange(blocks(mix_a))
    first_b = finish(chip_b, came_b)
    hid_b = active(first_b)
    mix_b = join_product(hid_b, swap(hid_b, 1), down, 0, place)
    slot_4, mix_b = tie(slot_4, mix_b)
    act0_a = plus(emb_a, slot_4)
    pass_a = across(act0_a)

    slot_5 = exchange(either(blocks(mix_b), spread(pass_a)))
    act0_b = plus(emb_b, slot_5)
    pass_b = across(act0_b)
    kept_a, sent_a = split_product(whole(slot_5), (up,), (0,), place)
    pass_b, kept_a, sent_a = tie(pass_b, kept_a, sent_a)
    slot_6 = exchange(spread(pass_b))
    chip_a, came_a = chip_sum(kept_a, sent_a)
    pre_a = finish(chip_a, came_a)
    back_a = slope(pre_a, first_b)
    mix_a = join_product(back_a, swap(back_a, 1), up, 1, place)
    slot_6, mix_a = tie(slot_6, mix_a)
    kept_b, sent_b = split_product(whole(slot_6), (up,), (0,), place)
    mix_a, kept_b, sent_b = tie(mix_a, kept_b, sent_b)
    slot_7 = exchange(blocks(mix_a))
    chip_b, came_b = chip_sum(kept_b, sent_b)
    hid_a = active(pre_a)
    out_a = join_product(hid_a, swap(hid_a, 1), down, 0, place)
    came_b, out_a = tie(came_b, out_a)
    pre_b = finish(chip_b, came_b)
    back_b = slope(pre_b, first_a)
    mix_b = join_product(back_b, swap(back_b, 1), up, 1, place)
    slot_7, mix_b = tie(slot_7, mix_b)
    grad1_a = plus(cotangent[0], slot_7)
    gone_a = across(grad1_a)
    slot_8 = exchange(either(spread(gone_a), blocks(mix_b)))
    hid_b = active(pre_b)
    out_b = join_product(hid_b, swap(hid_b, 1), down, 0, place)
    slot_8, out_b = tie(slot_8, out_b)

    grad1_b = plus(cotangent[1], slot_8)
    gone_b = across(grad1_b)
    kept_a, sent_a = split_product(whole(slot_8), (down,), (1,), place)
    gone_b, kept_a, sent_a = tie(gone_b, kept_a, sent_a)
    slot_9 = exchange(either(spread(gone_b), blocks(out_a)))
    chip_a, came_a = chip_sum(kept_a, sent_a)
    back_a = slope(first_a, finish(chip_a, came_a))
    mix_a = join_product(back_a, swap(back_a, 1), up, 1, place)
    slot_9, mix_a = tie(slot_9, mix_a)
    kept_b, sent_b = split_product(whole(slot_9), (down,), (1,), place)
    mix_a, kept_b, sent_b = tie(mix_a, kept_b, sent_b)
    slot_10 = exchange(either(blocks(mix_a), blocks(out_b)))
    act1_a = plus(pass_a, slot_9)
    chip_b, came_b = chip_sum(kept_b, sent_b)
    back_b = slope(first_b, finish(chip_b, came_b))
    mix_b = join_product(back_b, swap(back_b, 1), up, 1, place)
    slot_10, mix_b, act1_a = tie(slot_10, mix_b, act1_a)
    slot_11 = exchange(blocks(mix_b))
    act1_b = plus(pass_b, slot_10)
    grad0_a = plus(gone_a, slot_10)
    slot_11, act1_b, grad0_a = tie(slot_11, act1_b, grad0_a)
    grad0_b = plus(gone_b, slot_11)

    acts = jnp.stack([either(act0_a, act1_a), either(act0_b, act1_b)])
    grads = jnp.stack([either(grad0_a, grad1_a), either(grad0_b, grad1_b)])
    return (acts[None], grads[None])


def solution(mesh):
    return jax.shard_map(
        on_device,
        mesh=mesh,
        in_specs=(
            P(),
            P("dp", "mp"),
            P("segment", "mp", "dp"),
            P("segment", "dp", "mp"),
            P(None, "dp", "mp"),
        ),
        out_specs=(P("segment", None, "dp", "mp"), P("segment", None, "dp", "mp")),
        check_vma=False,
    )
```

```python
import functools

import jax
import jax.numpy as jnp
from jax import lax
from jax.experimental import pallas as pl
from jax.experimental.pallas import tpu as pltpu
from jax.sharding import PartitionSpec as P

root_coef = 0.7978845608028654
bf16, f32 = jnp.bfloat16, jnp.float32
tile = 512
cost = pl.CostEstimate(flops=200_000_000, bytes_accessed=1_000_000, transcendentals=0)
params = pltpu.CompilerParams(vmem_limit_bytes=44 * 1024 * 1024)


def gelu_value(value):
    return 0.5 * value * (1.0 + jnp.tanh(root_coef * (value + 0.044715 * value * value * value)))


def gelu_slope(value):
    inner = jnp.tanh(root_coef * (value + 0.044715 * value * value * value))
    return 0.5 * (1.0 + inner) + 0.5 * value * (1.0 - inner * inner) * root_coef * (
        1.0 + 0.134145 * value * value
    )


def swap(value, bit):
    return lax.ppermute(value, "mp", [(i, i ^ bit) for i in range(4)])


def across(value):
    return lax.ppermute(value, "segment", [(0, 1), (1, 0)])


def exchange(blocks):
    return lax.all_to_all(blocks, "dp", 0, 0)


def spread(own):
    return jnp.broadcast_to(own[None], (lax.axis_size("dp"),) + own.shape)


def collect(blocks):
    return jnp.sum(blocks.astype(f32), axis=0)


def plus(own, blocks):
    return (own.astype(f32) + collect(blocks)).astype(bf16)


def multiply(rows, weight, dim):
    return lax.dot_general(
        rows, weight, (((1,), (dim,)), ((), ())), preferred_element_type=f32
    )


def start_weight(weight, dim, held, arrived):
    copies = []
    for index in range(held.shape[0]):
        columns = pl.ds(index * tile, tile)
        source = weight.at[:, columns] if dim == 0 else weight.at[columns, :]
        copies.append(pltpu.make_async_copy(source, held.at[index], arrived.at[index]))
        copies[-1].start()
    return copies


def split_tiles(rows, copies, held, dim, low, staged_kept, staged_sent, kept, sent, left):
    half = kept.shape[0]
    pending = []
    for index, copy in enumerate(copies):
        copy.wait()
        total = multiply(rows[...], held[index], dim)
        staged_kept[index] = jnp.where(low, total[:half], total[half:])
        staged_sent[index] = jnp.where(low, total[half:], total[:half]).astype(bf16)
        columns = pl.ds(index * tile, tile)
        pending += [
            pltpu.make_async_copy(staged_sent.at[index], sent.at[:, columns], left.at[2 * index]),
            pltpu.make_async_copy(
                staged_kept.at[index], kept.at[:, columns], left.at[2 * index + 1]
            ),
        ]
        pending[-2].start()
        pending[-1].start()
    for copy in pending:
        copy.wait()


def held_shape(weight, dim):
    depth, count = weight.shape[dim], weight.shape[1 - dim]
    return (count // tile, depth, tile) if dim == 0 else (count // tile, tile, depth)


def split_kernel(dim, place, rows_in, weight, kept, sent, rows, *refs):
    staged_kept, staged_sent, arrived, left, held = refs
    rows_copy = pltpu.make_async_copy(rows_in, rows, arrived.at[arrived.shape[0] - 1])
    rows_copy.start()
    copies = start_weight(weight, dim, held, arrived)
    rows_copy.wait()
    low = place[0] == 0
    split_tiles(rows, copies, held, dim, low, staged_kept, staged_sent, kept, sent, left)


def enter_kernel(place, spot, slot_in, up, down, kept, sent, own, rows, *refs):
    staged_kept, staged_sent, arrived, left, held_up, held_down, slot = refs
    slot_copy = pltpu.make_async_copy(slot_in, slot, arrived.at[arrived.shape[0] - 1])
    slot_copy.start()
    low = place[0] == 0
    tok = own.shape[0] // 2

    def run(weight, dim, held):
        copies = start_weight(weight, dim, held, arrived)
        index = lax.broadcasted_iota(jnp.int32, (rows.shape[0], slot.shape[0]), 1)
        chosen = jnp.where(index == spot[...], 1.0, 0.0).astype(bf16)
        slot_copy.wait()
        rows[...] = multiply(chosen, slot[...], 0).astype(bf16)
        quarter = rows.shape[0] // 4
        first = place[2] * tok
        first = first + jnp.where(first >= quarter, quarter, 0)
        for m in range(2):
            begin = pl.multiple_of(first + m * quarter, tok)
            own[m * tok : (m + 1) * tok] = rows[pl.ds(begin, tok)]
        split_tiles(rows, copies, held, dim, low, staged_kept, staged_sent, kept, sent, left)

    @pl.when(place[1] == 0)
    def _():
        run(up, 0, held_up)

    @pl.when(place[1] != 0)
    def _():
        run(down, 1, held_down)


anywhere = pl.BlockSpec(memory_space=pl.ANY)
scalars = pl.BlockSpec(memory_space=pltpu.SMEM)
in_vmem = pl.BlockSpec(memory_space=pltpu.VMEM)


def split_parts(count, rows, depth):
    tiles, half = count // tile, rows // 2
    out = [jax.ShapeDtypeStruct((half, count), f32), jax.ShapeDtypeStruct((half, count), bf16)]
    scratch = [
        pltpu.VMEM((rows, depth), bf16),
        pltpu.VMEM((tiles, half, tile), f32),
        pltpu.VMEM((tiles, half, tile), bf16),
        pltpu.SemaphoreType.DMA((tiles + 1,)),
        pltpu.SemaphoreType.DMA((2 * tiles,)),
    ]
    return out, scratch


def split_product(rows, weight, dim, place):
    out, scratch = split_parts(weight.shape[1 - dim], *rows.shape)
    return pl.pallas_call(
        functools.partial(split_kernel, dim),
        in_specs=[scalars, anywhere, anywhere],
        out_specs=[anywhere, anywhere],
        out_shape=out,
        scratch_shapes=scratch + [pltpu.VMEM(held_shape(weight, dim), bf16)],
        compiler_params=params,
        cost_estimate=cost,
    )(place, rows, weight)


def enter_product(spot, slot, up, down, tok, place):
    out, scratch = split_parts(up.shape[1], spot.shape[0], slot.shape[1])
    return pl.pallas_call(
        enter_kernel,
        in_specs=[scalars, in_vmem, anywhere, anywhere, anywhere],
        out_specs=[anywhere, anywhere, in_vmem],
        out_shape=out + [jax.ShapeDtypeStruct((2 * tok, slot.shape[1]), bf16)],
        scratch_shapes=scratch
        + [
            pltpu.VMEM(held_shape(up, 0), bf16),
            pltpu.VMEM(held_shape(down, 1), bf16),
            pltpu.VMEM(slot.shape, bf16),
        ],
        compiler_params=params,
        cost_estimate=cost,
    )(place, spot, slot, up, down)


def rank_kernel(table_rows, place, row_ids, column_ids, spot, wanted, most):
    count, capacity = spot.shape[0], wanted.shape[0]
    shift = table_rows.bit_length() - 1
    across_ids, down_ids = row_ids[...], column_ids[...]
    here = lax.broadcasted_iota(jnp.int32, (count, count), 0)
    there = lax.broadcasted_iota(jnp.int32, (count, count), 1)
    equal = across_ids == down_ids
    same = (across_ids >> shift) == (down_ids >> shift)

    def ones(mask):
        return jnp.where(mask, 1.0, 0.0)

    repeat_down = jnp.sum(ones(equal & (there < here)), axis=1, keepdims=True)
    repeat_across = jnp.sum(ones(equal & (here < there)), axis=0, keepdims=True)
    number = jnp.sum(
        ones(same & (here < there) & (repeat_down == 0.0)), axis=0, keepdims=True
    )
    mine = jnp.sum(
        jnp.where(equal & (repeat_across == 0.0), number, 0.0), axis=1, keepdims=True
    )
    spot[...] = (down_ids >> shift) * capacity + mine.astype(jnp.int32)
    slot = lax.broadcasted_iota(jnp.int32, (capacity, count), 0)
    local = across_ids - (place[2] << shift)
    named = (
        (local >= 0)
        & (local < table_rows)
        & (repeat_across == 0.0)
        & (number.astype(jnp.int32) == slot)
    )
    wanted[...] = (
        jnp.sum(jnp.where(named, local.astype(f32) + 1.0, 0.0), axis=1, keepdims=True) - 1.0
    ).astype(jnp.int32)
    most[...] = jnp.max(mine, axis=0, keepdims=True).astype(jnp.int32) + 1


def rank(ids, table_rows, capacity, place):
    count = ids.shape[0]
    return pl.pallas_call(
        functools.partial(rank_kernel, table_rows),
        in_specs=[scalars, in_vmem, in_vmem],
        out_specs=[in_vmem] * 3,
        out_shape=[
            jax.ShapeDtypeStruct((count, 1), jnp.int32),
            jax.ShapeDtypeStruct((capacity, 1), jnp.int32),
            jax.ShapeDtypeStruct((1, 1), jnp.int32),
        ],
        compiler_params=params,
        cost_estimate=cost,
    )(place, ids[None, :], ids[:, None])


def join_kernel(dim, place, mine, other, weight, out, rows, staged, arrived, left, held):
    half = mine.shape[0]
    tiles = held.shape[0]
    parts = [
        pltpu.make_async_copy(
            part,
            rows.at[pl.ds(pl.multiple_of(position * half, half), half)],
            arrived.at[tiles + index],
        )
        for index, (part, position) in enumerate(((mine, place[0]), (other, 1 - place[0])))
    ]
    for copy in parts:
        copy.start()
    copies = start_weight(weight, dim, held, arrived)
    for copy in parts:
        copy.wait()
    pending = []
    for index, copy in enumerate(copies):
        copy.wait()
        staged[index] = multiply(rows[...], held[index], dim).astype(bf16)
        pending.append(
            pltpu.make_async_copy(
                staged.at[index], out.at[:, pl.ds(index * tile, tile)], left.at[index]
            )
        )
        pending[-1].start()
    for copy in pending:
        copy.wait()


def join_product(mine, other, weight, dim, place):
    count = weight.shape[1 - dim]
    tiles = count // tile
    half, depth = mine.shape
    return pl.pallas_call(
        functools.partial(join_kernel, dim),
        in_specs=[scalars] + [anywhere] * 3,
        out_specs=anywhere,
        out_shape=jax.ShapeDtypeStruct((2 * half, count), bf16),
        scratch_shapes=[
            pltpu.VMEM((2 * half, depth), bf16),
            pltpu.VMEM((tiles, 2 * half, tile), bf16),
            pltpu.SemaphoreType.DMA((tiles + 2,)),
            pltpu.SemaphoreType.DMA((tiles,)),
            pltpu.VMEM(held_shape(weight, dim), bf16),
        ],
        compiler_params=params,
        cost_estimate=cost,
    )(place, mine, other, weight)


def lookup_kernel(wanted, table, out, chosen):
    @pl.when(pl.program_id(0) == 0)
    def _():
        row = lax.broadcasted_iota(jnp.int32, chosen.shape, 1)
        chosen[...] = jnp.where(row == wanted[...], 1.0, 0.0).astype(bf16)

    out[...] = multiply(chosen[...], table[...], 0).astype(bf16)


def lookup(wanted, table):
    count = wanted.shape[0]
    rows, feat = table.shape
    return pl.pallas_call(
        lookup_kernel,
        grid=(feat // tile,),
        in_specs=[
            pl.BlockSpec(wanted.shape, lambda i: (0, 0)),
            pl.BlockSpec((rows, tile), lambda i: (0, i)),
        ],
        out_specs=pl.BlockSpec((count, tile), lambda i: (0, i)),
        scratch_shapes=[pltpu.VMEM((count, rows), bf16)],
        out_shape=jax.ShapeDtypeStruct((count, feat), bf16),
        compiler_params=params,
        cost_estimate=cost,
    )(wanted, table)


def tie(*values):
    return lax.optimization_barrier(values)


def after(value, *earlier):
    return lax.optimization_barrier((value, *earlier))[0]


def on_device(token_ids, table, w_up, w_down, cotangent):
    micro, tok, feat = cotangent.shape
    dp = lax.axis_size("dp")
    up = w_up[0]
    down = w_down[0]
    is_first = lax.axis_index("segment") == 0
    here = lax.axis_index("dp")
    place = jnp.stack(
        [lax.axis_index("mp") % 2, lax.axis_index("segment"), here]
    ).astype(jnp.int32)
    capacity = micro * tok
    table_rows = table.shape[0]
    own_cot = cotangent.reshape(capacity, feat)

    def whole(slot):
        return slot.reshape(-1, feat)

    def blocks(rows):
        return rows.reshape(dp, -1, feat)

    def either(left, right):
        return jnp.where(is_first, left, right)

    def chip_sum(kept, sent):
        chip = kept + swap(sent, 1).astype(f32)
        return chip, chip.astype(bf16)

    def finish(chip, came):
        return chip + came.astype(f32)

    def active(summed):
        return gelu_value(summed).astype(bf16)

    spot, wanted, most = rank(token_ids.reshape(-1), table_rows, capacity, place)
    fits = most[0, 0] <= capacity

    def sparse():
        return lookup(wanted, table)

    def dense():
        by_owner = token_ids.reshape(micro, dp, tok).transpose(1, 0, 2).reshape(-1, 1)
        fetched = lookup(by_owner - here * table_rows, table)
        return collect(exchange(blocks(fetched))).astype(bf16)

    found = lax.cond(fits, sparse, dense)
    slot_2 = whole(exchange(spread(either(found, own_cot))))
    token = jnp.arange(micro * dp * tok, dtype=jnp.int32)
    in_order = (token // tok % dp) * capacity + token // (dp * tok) * tok + token % tok
    spot = jnp.where(is_first & fits, spot, in_order[:, None])
    spot = spot.reshape(micro, 2, -1).transpose(1, 0, 2).reshape(-1, 1)

    kept, sent, embedded = enter_product(spot, slot_2, up, down, tok, place)
    chip, send = chip_sum(kept, sent)
    half = chip.shape[0] // 2
    emb_a, emb_b = embedded[:tok], embedded[tok:]
    came_a, came_b = swap(send[:half], 2), swap(send[half:], 2)
    first_a = finish(chip[:half], came_a)
    hid_a = active(first_a)
    mix_a = join_product(hid_a, swap(hid_a, 1), down, 0, place)
    slot_4 = exchange(blocks(mix_a))
    act0_a = plus(emb_a, slot_4)
    pass_a = across(act0_a)
    first_b = finish(chip[half:], after(came_b, act0_a))
    hid_b = active(first_b)
    mix_b = join_product(hid_b, swap(hid_b, 1), down, 0, place)

    slot_5 = exchange(after(either(blocks(mix_b), spread(pass_a)), slot_4))
    slope_a = gelu_slope(after(first_a, mix_b))
    slope_b = gelu_slope(after(first_b, mix_b))
    slot_5 = after(slot_5, slope_a, slope_b)
    act0_b = plus(emb_b, slot_5)
    pass_b = across(act0_b)
    kept_a, sent_a = split_product(whole(after(slot_5, act0_b)), up, 0, place)
    pass_b, kept_a, sent_a = tie(pass_b, kept_a, sent_a)
    chip_a, send_a = chip_sum(kept_a, sent_a)
    came_a = swap(send_a, 2)
    slot_6 = exchange(after(spread(after(pass_b, kept_a)), slot_5))
    pre_a = finish(chip_a, came_a)
    back_a = (gelu_slope(pre_a) * first_a).astype(bf16)
    mix_a = join_product(back_a, swap(back_a, 1), up, 1, place)
    kept_b, sent_b = split_product(whole(after(slot_6, mix_a)), up, 0, place)
    slot_7 = exchange(after(blocks(mix_a), slot_6, kept_b))
    chip_b, send_b = chip_sum(kept_b, sent_b)
    came_b = swap(send_b, 2)
    hid_a = active(after(pre_a, send_b))
    out_a = join_product(hid_a, swap(hid_a, 1), down, 0, place)
    pre_b = finish(chip_b, after(came_b, out_a))
    back_b = (gelu_slope(pre_b) * first_b).astype(bf16)
    grad1_a = plus(cotangent[0], after(slot_7, back_b))
    gone_a = across(grad1_a)
    mix_b = join_product(after(back_b, grad1_a), swap(back_b, 1), up, 1, place)
    slot_8 = exchange(
        after(either(spread(after(gone_a, mix_b)), blocks(mix_b)), slot_7)
    )
    hid_b = active(after(pre_b, mix_b))
    out_b = join_product(hid_b, swap(hid_b, 1), down, 0, place)
    slot_8 = after(slot_8, out_b)

    grad1_b = plus(cotangent[1], slot_8)
    gone_b = across(grad1_b)
    kept_a, sent_a = split_product(whole(after(slot_8, grad1_b)), down, 1, place)
    gone_b, kept_a, sent_a = tie(gone_b, kept_a, sent_a)
    chip_a, send_a = chip_sum(kept_a, sent_a)
    came_a = swap(send_a, 2)
    slot_9 = exchange(
        after(either(spread(after(gone_b, kept_a)), blocks(out_a)), slot_8)
    )
    back_a = (slope_a * finish(chip_a, came_a)).astype(bf16)
    far_a = swap(back_a, 1)
    kept_b, sent_b = split_product(whole(after(slot_9, back_a)), down, 1, place)
    chip_b, send_b = chip_sum(kept_b, sent_b)
    came_b = swap(send_b, 2)
    mix_a = join_product(after(back_a, send_b), far_a, up, 1, place)
    slot_10 = exchange(after(either(blocks(mix_a), blocks(out_b)), slot_9))
    act1_a = plus(pass_a, after(slot_9, mix_a))
    back_b = (slope_b * finish(chip_b, after(came_b, act1_a))).astype(bf16)
    mix_b = join_product(back_b, swap(back_b, 1), up, 1, place)
    slot_11 = exchange(after(blocks(mix_b), slot_10))
    act1_b = plus(pass_b, slot_10)
    grad0_a = plus(gone_a, slot_10)
    grad0_b = plus(gone_b, after(slot_11, act1_b, grad0_a))

    acts = jnp.stack([either(act0_a, act1_a), either(act0_b, act1_b)])
    grads = jnp.stack([either(grad0_a, grad1_a), either(grad0_b, grad1_b)])
    return (acts[None], grads[None])


def solution(mesh):
    return jax.shard_map(
        on_device,
        mesh=mesh,
        in_specs=(
            P(),
            P("dp", "mp"),
            P("segment", "mp", "dp"),
            P("segment", "dp", "mp"),
            P(None, "dp", "mp"),
        ),
        out_specs=(P("segment", None, "dp", "mp"), P("segment", None, "dp", "mp")),
        check_vma=False,
    )
```

```python
import functools

import jax
import jax.numpy as jnp
from jax import lax
from jax.experimental import pallas as pl
from jax.experimental.pallas import tpu as pltpu
from jax.sharding import PartitionSpec as P

root_coef = 0.7978845608028654
bf16, f32 = jnp.bfloat16, jnp.float32
tile = 512
cost = pl.CostEstimate(flops=200_000_000, bytes_accessed=1_000_000, transcendentals=0)
params = pltpu.CompilerParams(vmem_limit_bytes=44 * 1024 * 1024)


def gelu_value(value):
    return 0.5 * value * (1.0 + jnp.tanh(root_coef * (value + 0.044715 * value * value * value)))


def gelu_slope(value):
    inner = jnp.tanh(root_coef * (value + 0.044715 * value * value * value))
    return 0.5 * (1.0 + inner) + 0.5 * value * (1.0 - inner * inner) * root_coef * (
        1.0 + 0.134145 * value * value
    )


def swap(value, bit):
    return lax.ppermute(value, "mp", [(i, i ^ bit) for i in range(4)])


def across(value):
    return lax.ppermute(value, "segment", [(0, 1), (1, 0)])


def exchange(blocks):
    return lax.all_to_all(blocks, "dp", 0, 0)


def spread(own):
    return jnp.broadcast_to(own[None], (lax.axis_size("dp"),) + own.shape)


def collect(blocks):
    return jnp.sum(blocks.astype(f32), axis=0)


def plus(own, blocks):
    return (own.astype(f32) + collect(blocks)).astype(bf16)


def multiply(rows, weight, dim):
    return lax.dot_general(
        rows, weight, (((1,), (dim,)), ((), ())), preferred_element_type=f32
    )


def start_weight(weight, dim, held, arrived):
    copies = []
    for index in range(held.shape[0]):
        columns = pl.ds(index * tile, tile)
        source = weight.at[:, columns] if dim == 0 else weight.at[columns, :]
        copies.append(pltpu.make_async_copy(source, held.at[index], arrived.at[index]))
        copies[-1].start()
    return copies


def split_tiles(rows, copies, held, dim, low, staged_kept, staged_sent, kept, sent, left):
    half = kept.shape[0]
    pending = []
    for index, copy in enumerate(copies):
        copy.wait()
        total = multiply(rows[...], held[index], dim)
        staged_kept[index] = jnp.where(low, total[:half], total[half:]).astype(bf16)
        staged_sent[index] = jnp.where(low, total[half:], total[:half]).astype(bf16)
        columns = pl.ds(index * tile, tile)
        pending += [
            pltpu.make_async_copy(staged_sent.at[index], sent.at[:, columns], left.at[2 * index]),
            pltpu.make_async_copy(
                staged_kept.at[index], kept.at[:, columns], left.at[2 * index + 1]
            ),
        ]
        pending[-2].start()
        pending[-1].start()
    for copy in pending:
        copy.wait()


def held_shape(weight, dim):
    depth, count = weight.shape[dim], weight.shape[1 - dim]
    return (count // tile, depth, tile) if dim == 0 else (count // tile, tile, depth)


def split_kernel(dim, place, rows_in, weight, kept, sent, rows, *refs):
    staged_kept, staged_sent, arrived, left, held = refs
    rows_copy = pltpu.make_async_copy(rows_in, rows, arrived.at[arrived.shape[0] - 1])
    rows_copy.start()
    copies = start_weight(weight, dim, held, arrived)
    rows_copy.wait()
    low = place[0] == 0
    split_tiles(rows, copies, held, dim, low, staged_kept, staged_sent, kept, sent, left)


def enter_kernel(place, spot, slot_in, up, down, kept, sent, own, rows, *refs):
    staged_kept, staged_sent, arrived, left, held_up, held_down, slot = refs
    slot_copy = pltpu.make_async_copy(slot_in, slot, arrived.at[arrived.shape[0] - 1])
    slot_copy.start()
    low = place[0] == 0
    tok = own.shape[0] // 2

    def run(weight, dim, held):
        copies = start_weight(weight, dim, held, arrived)
        index = lax.broadcasted_iota(jnp.int32, (rows.shape[0], slot.shape[0]), 1)
        chosen = jnp.where(index == spot[...], 1.0, 0.0).astype(bf16)
        slot_copy.wait()
        rows[...] = multiply(chosen, slot[...], 0).astype(bf16)
        quarter = rows.shape[0] // 4
        first = place[2] * tok
        first = first + jnp.where(first >= quarter, quarter, 0)
        for m in range(2):
            begin = pl.multiple_of(first + m * quarter, tok)
            own[m * tok : (m + 1) * tok] = rows[pl.ds(begin, tok)]
        split_tiles(rows, copies, held, dim, low, staged_kept, staged_sent, kept, sent, left)

    @pl.when(place[1] == 0)
    def _():
        run(up, 0, held_up)

    @pl.when(place[1] != 0)
    def _():
        run(down, 1, held_down)


anywhere = pl.BlockSpec(memory_space=pl.ANY)
scalars = pl.BlockSpec(memory_space=pltpu.SMEM)
in_vmem = pl.BlockSpec(memory_space=pltpu.VMEM)


def split_parts(count, rows, depth):
    tiles, half = count // tile, rows // 2
    out = [jax.ShapeDtypeStruct((half, count), bf16)] * 2
    scratch = [
        pltpu.VMEM((rows, depth), bf16),
        pltpu.VMEM((tiles, half, tile), bf16),
        pltpu.VMEM((tiles, half, tile), bf16),
        pltpu.SemaphoreType.DMA((tiles + 1,)),
        pltpu.SemaphoreType.DMA((2 * tiles,)),
    ]
    return out, scratch


def split_product(rows, weight, dim, place):
    out, scratch = split_parts(weight.shape[1 - dim], *rows.shape)
    return pl.pallas_call(
        functools.partial(split_kernel, dim),
        in_specs=[scalars, anywhere, anywhere],
        out_specs=[anywhere, anywhere],
        out_shape=out,
        scratch_shapes=scratch + [pltpu.VMEM(held_shape(weight, dim), bf16)],
        compiler_params=params,
        cost_estimate=cost,
    )(place, rows, weight)


def enter_product(spot, slot, up, down, tok, place):
    out, scratch = split_parts(up.shape[1], spot.shape[0], slot.shape[1])
    return pl.pallas_call(
        enter_kernel,
        in_specs=[scalars, in_vmem, anywhere, anywhere, anywhere],
        out_specs=[anywhere, anywhere, in_vmem],
        out_shape=out + [jax.ShapeDtypeStruct((2 * tok, slot.shape[1]), bf16)],
        scratch_shapes=scratch
        + [
            pltpu.VMEM(held_shape(up, 0), bf16),
            pltpu.VMEM(held_shape(down, 1), bf16),
            pltpu.VMEM(slot.shape, bf16),
        ],
        compiler_params=params,
        cost_estimate=cost,
    )(place, spot, slot, up, down)


def rank_kernel(table_rows, place, row_ids, column_ids, spot, wanted, most):
    count, capacity = spot.shape[0], wanted.shape[0]
    shift = table_rows.bit_length() - 1
    across_ids, down_ids = row_ids[...], column_ids[...]
    here = lax.broadcasted_iota(jnp.int32, (count, count), 0)
    there = lax.broadcasted_iota(jnp.int32, (count, count), 1)
    equal = across_ids == down_ids
    same = (across_ids >> shift) == (down_ids >> shift)

    def ones(mask):
        return jnp.where(mask, 1.0, 0.0)

    repeat_down = jnp.sum(ones(equal & (there < here)), axis=1, keepdims=True)
    repeat_across = jnp.sum(ones(equal & (here < there)), axis=0, keepdims=True)
    number = jnp.sum(
        ones(same & (here < there) & (repeat_down == 0.0)), axis=0, keepdims=True
    )
    mine = jnp.sum(
        jnp.where(equal & (repeat_across == 0.0), number, 0.0), axis=1, keepdims=True
    )
    spot[...] = (down_ids >> shift) * capacity + mine.astype(jnp.int32)
    slot = lax.broadcasted_iota(jnp.int32, (capacity, count), 0)
    local = across_ids - (place[2] << shift)
    named = (
        (local >= 0)
        & (local < table_rows)
        & (repeat_across == 0.0)
        & (number.astype(jnp.int32) == slot)
    )
    wanted[...] = (
        jnp.sum(jnp.where(named, local.astype(f32) + 1.0, 0.0), axis=1, keepdims=True) - 1.0
    ).astype(jnp.int32)
    most[...] = jnp.max(mine, axis=0, keepdims=True).astype(jnp.int32) + 1


def rank(ids, table_rows, capacity, place):
    count = ids.shape[0]
    return pl.pallas_call(
        functools.partial(rank_kernel, table_rows),
        in_specs=[scalars, in_vmem, in_vmem],
        out_specs=[in_vmem] * 3,
        out_shape=[
            jax.ShapeDtypeStruct((count, 1), jnp.int32),
            jax.ShapeDtypeStruct((capacity, 1), jnp.int32),
            jax.ShapeDtypeStruct((1, 1), jnp.int32),
        ],
        compiler_params=params,
        cost_estimate=cost,
    )(place, ids[None, :], ids[:, None])


def join_kernel(dim, swapped, place, mine, other, weight, *refs):
    if swapped:
        instead, refs = refs[0], refs[1:]
    out, rows, staged, arrived, left, held = refs
    half = mine.shape[0]
    tiles = held.shape[0]

    def run():
        parts = [
            pltpu.make_async_copy(
                part,
                rows.at[pl.ds(pl.multiple_of(position * half, half), half)],
                arrived.at[tiles + index],
            )
            for index, (part, position) in enumerate(((mine, place[0]), (other, 1 - place[0])))
        ]
        for copy in parts:
            copy.start()
        copies = start_weight(weight, dim, held, arrived)
        for copy in parts:
            copy.wait()
        pending = []
        for index, copy in enumerate(copies):
            copy.wait()
            staged[index] = multiply(rows[...], held[index], dim).astype(bf16)
            pending.append(
                pltpu.make_async_copy(
                    staged.at[index], out.at[:, pl.ds(index * tile, tile)], left.at[index]
                )
            )
            pending[-1].start()
        for copy in pending:
            copy.wait()

    if swapped:
        pl.when(place[1] == 0)(run)

        @pl.when(place[1] != 0)
        def _():
            copy = pltpu.make_async_copy(instead, out, left.at[0])
            copy.start()
            copy.wait()

    else:
        run()


def join_product(mine, other, weight, dim, place, instead=()):
    count = weight.shape[1 - dim]
    tiles = count // tile
    half, depth = mine.shape
    return pl.pallas_call(
        functools.partial(join_kernel, dim, bool(instead)),
        in_specs=[scalars] + [anywhere] * (3 + len(instead)),
        out_specs=anywhere,
        out_shape=jax.ShapeDtypeStruct((2 * half, count), bf16),
        scratch_shapes=[
            pltpu.VMEM((2 * half, depth), bf16),
            pltpu.VMEM((tiles, 2 * half, tile), bf16),
            pltpu.SemaphoreType.DMA((tiles + 2,)),
            pltpu.SemaphoreType.DMA((tiles,)),
            pltpu.VMEM(held_shape(weight, dim), bf16),
        ],
        compiler_params=params,
        cost_estimate=cost,
    )(place, mine, other, weight, *instead)


def lookup_kernel(wanted, table, out, chosen):
    @pl.when(pl.program_id(0) == 0)
    def _():
        row = lax.broadcasted_iota(jnp.int32, chosen.shape, 1)
        chosen[...] = jnp.where(row == wanted[...], 1.0, 0.0).astype(bf16)

    out[...] = multiply(chosen[...], table[...], 0).astype(bf16)


def lookup(wanted, table):
    count = wanted.shape[0]
    rows, feat = table.shape
    return pl.pallas_call(
        lookup_kernel,
        grid=(feat // tile,),
        in_specs=[
            pl.BlockSpec(wanted.shape, lambda i: (0, 0)),
            pl.BlockSpec((rows, tile), lambda i: (0, i)),
        ],
        out_specs=pl.BlockSpec((count, tile), lambda i: (0, i)),
        scratch_shapes=[pltpu.VMEM((count, rows), bf16)],
        out_shape=jax.ShapeDtypeStruct((count, feat), bf16),
        compiler_params=params,
        cost_estimate=cost,
    )(wanted, table)


def tie(*values):
    return lax.optimization_barrier(values)


def after(value, *earlier):
    return lax.optimization_barrier((value, *earlier))[0]


def on_device(token_ids, table, w_up, w_down, cotangent):
    micro, tok, feat = cotangent.shape
    dp = lax.axis_size("dp")
    up = w_up[0]
    down = w_down[0]
    is_first = lax.axis_index("segment") == 0
    here = lax.axis_index("dp")
    place = jnp.stack(
        [lax.axis_index("mp") % 2, lax.axis_index("segment"), here]
    ).astype(jnp.int32)
    capacity = micro * tok
    table_rows = table.shape[0]
    own_cot = cotangent.reshape(capacity, feat)

    def whole(slot):
        return slot.reshape(-1, feat)

    def blocks(rows):
        return rows.reshape(dp, -1, feat)

    def either(left, right):
        return jnp.where(is_first, left, right)

    def chip_sum(kept, sent):
        return (kept.astype(f32) + swap(sent, 1).astype(f32)).astype(bf16)

    def finish(chip, came):
        return chip.astype(f32) + came.astype(f32)

    def active(summed):
        return gelu_value(summed.astype(f32)).astype(bf16)

    def slope(saved, summed):
        return (gelu_slope(saved) * summed.astype(f32)).astype(bf16)

    spot, wanted, most = rank(token_ids.reshape(-1), table_rows, capacity, place)
    fits = most[0, 0] <= capacity

    def sparse():
        return lookup(wanted, table)

    def dense():
        by_owner = token_ids.reshape(micro, dp, tok).transpose(1, 0, 2).reshape(-1, 1)
        fetched = lookup(by_owner - here * table_rows, table)
        return collect(exchange(blocks(fetched))).astype(bf16)

    found = lax.cond(fits, sparse, dense)
    slot_2 = whole(exchange(spread(either(found, own_cot))))
    token = jnp.arange(micro * dp * tok, dtype=jnp.int32)
    in_order = (token // tok % dp) * capacity + token // (dp * tok) * tok + token % tok
    spot = jnp.where(is_first & fits, spot, in_order[:, None])
    spot = spot.reshape(micro, 2, -1).transpose(1, 0, 2).reshape(-1, 1)

    kept, sent, embedded = enter_product(spot, slot_2, up, down, tok, place)
    chip = chip_sum(kept, sent)
    half = chip.shape[0] // 2
    emb_a, emb_b = embedded[:tok], embedded[tok:]
    came_a, came_b = swap(chip[:half], 2), swap(chip[half:], 2)
    first_a = finish(chip[:half], came_a)
    hid_a, first_a = active(first_a), first_a.astype(bf16)
    mix_a = join_product(hid_a, swap(hid_a, 1), down, 0, place)
    slot_4 = exchange(blocks(mix_a))
    first_b = finish(chip[half:], after(came_b, mix_a))
    hid_b, first_b = active(first_b), first_b.astype(bf16)
    act0_a = plus(emb_a, after(slot_4, hid_b))
    pass_a = across(act0_a)
    hid_b = after(hid_b, act0_a)
    mix_b = join_product(hid_b, swap(hid_b, 1), down, 0, place)

    slot_5 = exchange(after(either(blocks(mix_b), spread(pass_a)), slot_4))
    slope_a = gelu_slope(after(first_a, mix_b).astype(f32)).astype(bf16)
    slope_b = gelu_slope(after(first_b, mix_b).astype(f32)).astype(bf16)
    slot_5 = after(slot_5, slope_a, slope_b)
    act0_b = plus(emb_b, slot_5)
    pass_b = across(act0_b)
    kept_a, sent_a = split_product(whole(after(slot_5, act0_b)), up, 0, place)
    pass_b, kept_a, sent_a = tie(pass_b, kept_a, sent_a)
    chip_a = chip_sum(kept_a, sent_a)
    came_a = swap(chip_a, 2)
    slot_6 = exchange(after(spread(after(pass_b, kept_a)), slot_5))
    pre_a = finish(chip_a, came_a)
    back_a = slope(pre_a, first_a)
    pre_a = pre_a.astype(bf16)
    mix_a = join_product(back_a, swap(back_a, 1), up, 1, place)
    kept_b, sent_b = split_product(whole(after(slot_6, mix_a)), up, 0, place)
    slot_7 = exchange(after(blocks(mix_a), slot_6))
    chip_b = chip_sum(kept_b, sent_b)
    came_b = swap(chip_b, 2)
    hid_a = active(after(pre_a, chip_b))
    out_a = join_product(hid_a, swap(hid_a, 1), down, 0, place)
    grad1_a = plus(cotangent[0], after(slot_7, out_a))
    gone_a = across(grad1_a)
    pre_b = finish(chip_b, after(came_b, grad1_a))
    back_b = slope(pre_b, first_b)
    pre_b = pre_b.astype(bf16)
    mix_b = join_product(back_b, swap(back_b, 1), up, 1, place)
    slot_8 = exchange(
        after(either(spread(after(gone_a, mix_b)), blocks(mix_b)), slot_7)
    )
    hid_b = active(after(pre_b, mix_b))
    out_b = join_product(hid_b, swap(hid_b, 1), down, 0, place)
    slot_8 = after(slot_8, out_b)

    grad1_b = plus(cotangent[1], slot_8)
    gone_b = across(grad1_b)
    kept_a, sent_a = split_product(whole(after(slot_8, grad1_b)), down, 1, place)
    send_9 = either(spread(gone_b), blocks(out_a))
    send_9, kept_a, sent_a = tie(send_9, kept_a, sent_a)
    slot_9 = exchange(after(send_9, slot_8))
    chip_a = chip_sum(kept_a, sent_a)
    came_a = swap(chip_a, 2)
    kept_b, sent_b = split_product(whole(slot_9), down, 1, place)
    back_a = (slope_a.astype(f32) * finish(chip_a, after(came_a, kept_b))).astype(bf16)
    far_a = swap(back_a, 1)
    chip_b = chip_sum(kept_b, sent_b)
    came_b = swap(chip_b, 2)
    mix_a = join_product(after(back_a, chip_b), far_a, up, 1, place, (out_b,))
    slot_10 = exchange(after(blocks(mix_a), slot_9))
    act1_a = plus(pass_a, after(slot_9, mix_a))
    back_b = (slope_b.astype(f32) * finish(chip_b, after(came_b, act1_a))).astype(bf16)
    mix_b = join_product(back_b, swap(back_b, 1), up, 1, place)
    slot_11 = exchange(after(blocks(mix_b), slot_10))
    act1_b = plus(pass_b, slot_10)
    grad0_a = plus(gone_a, slot_10)
    grad0_b = plus(gone_b, after(slot_11, act1_b, grad0_a))

    acts = jnp.stack([either(act0_a, act1_a), either(act0_b, act1_b)])
    grads = jnp.stack([either(grad0_a, grad1_a), either(grad0_b, grad1_b)])
    return (acts[None], grads[None])


def solution(mesh):
    return jax.shard_map(
        on_device,
        mesh=mesh,
        in_specs=(
            P(),
            P("dp", "mp"),
            P("segment", "mp", "dp"),
            P("segment", "dp", "mp"),
            P(None, "dp", "mp"),
        ),
        out_specs=(P("segment", None, "dp", "mp"), P("segment", None, "dp", "mp")),
        check_vma=False,
    )
```

```python
import functools

import jax
import jax.numpy as jnp
from jax import lax
from jax.experimental import pallas as pl
from jax.experimental.pallas import tpu as pltpu
from jax.sharding import PartitionSpec as P

root_coef = 0.7978845608028654
bf16, f32 = jnp.bfloat16, jnp.float32
tile = 512
cost = pl.CostEstimate(flops=200_000_000, bytes_accessed=1_000_000, transcendentals=0)
params = pltpu.CompilerParams(vmem_limit_bytes=44 * 1024 * 1024)


def gelu_value(value):
    return 0.5 * value * (1.0 + jnp.tanh(root_coef * (value + 0.044715 * value * value * value)))


def gelu_slope(value):
    inner = jnp.tanh(root_coef * (value + 0.044715 * value * value * value))
    return 0.5 * (1.0 + inner) + 0.5 * value * (1.0 - inner * inner) * root_coef * (
        1.0 + 0.134145 * value * value
    )


def swap(value, bit):
    return lax.ppermute(value, "mp", [(i, i ^ bit) for i in range(4)])


def across(value):
    return lax.ppermute(value, "segment", [(0, 1), (1, 0)])


def exchange(blocks):
    return lax.all_to_all(blocks, "dp", 0, 0)


def spread(own):
    return jnp.broadcast_to(own[None], (lax.axis_size("dp"),) + own.shape)


def collect(blocks):
    return jnp.sum(blocks.astype(f32), axis=0)


def plus(own, blocks):
    return (own.astype(f32) + collect(blocks)).astype(bf16)


def multiply(rows, weight, dim):
    return lax.dot_general(
        rows, weight, (((1,), (dim,)), ((), ())), preferred_element_type=f32
    )


def start_weight(weight, dim, held, arrived):
    copies = []
    for index in range(held.shape[0]):
        columns = pl.ds(index * tile, tile)
        source = weight.at[:, columns] if dim == 0 else weight.at[columns, :]
        copies.append(pltpu.make_async_copy(source, held.at[index], arrived.at[index]))
        copies[-1].start()
    return copies


def split_tiles(rows, copies, held, dim, low, staged_kept, staged_sent, kept, sent, left):
    half = kept.shape[0]
    for index, copy in enumerate(copies):
        copy.wait()
        total = multiply(rows[...], held[index], dim)
        columns = slice(index * tile, (index + 1) * tile)
        staged_kept[:, columns] = jnp.where(low, total[:half], total[half:]).astype(bf16)
        staged_sent[:, columns] = jnp.where(low, total[half:], total[:half]).astype(bf16)
    pending = [
        pltpu.make_async_copy(staged_sent, sent, left.at[0]),
        pltpu.make_async_copy(staged_kept, kept, left.at[1]),
    ]
    for copy in pending:
        copy.start()
    for copy in pending:
        copy.wait()


def held_shape(weight, dim):
    depth, count = weight.shape[dim], weight.shape[1 - dim]
    return (count // tile, depth, tile) if dim == 0 else (count // tile, tile, depth)


def split_kernel(dim, place, rows_in, weight, kept, sent, rows, *refs):
    staged_kept, staged_sent, arrived, left, held = refs
    rows_copy = pltpu.make_async_copy(rows_in, rows, arrived.at[arrived.shape[0] - 1])
    rows_copy.start()
    copies = start_weight(weight, dim, held, arrived)
    rows_copy.wait()
    low = place[0] == 0
    split_tiles(rows, copies, held, dim, low, staged_kept, staged_sent, kept, sent, left)


def enter_kernel(place, spot, slot_in, up, down, kept, sent, own, rows, *refs):
    staged_kept, staged_sent, arrived, left, held_up, held_down, slot = refs
    slot_copy = pltpu.make_async_copy(slot_in, slot, arrived.at[arrived.shape[0] - 1])
    slot_copy.start()
    low = place[0] == 0
    tok = own.shape[0] // 2

    def run(weight, dim, held):
        copies = start_weight(weight, dim, held, arrived)
        index = lax.broadcasted_iota(jnp.int32, (rows.shape[0], slot.shape[0]), 1)
        chosen = jnp.where(index == spot[...], 1.0, 0.0).astype(bf16)
        slot_copy.wait()
        rows[...] = multiply(chosen, slot[...], 0).astype(bf16)
        quarter = rows.shape[0] // 4
        first = place[2] * tok
        first = first + jnp.where(first >= quarter, quarter, 0)
        for m in range(2):
            begin = pl.multiple_of(first + m * quarter, tok)
            own[m * tok : (m + 1) * tok] = rows[pl.ds(begin, tok)]
        split_tiles(rows, copies, held, dim, low, staged_kept, staged_sent, kept, sent, left)

    @pl.when(place[1] == 0)
    def _():
        run(up, 0, held_up)

    @pl.when(place[1] != 0)
    def _():
        run(down, 1, held_down)


anywhere = pl.BlockSpec(memory_space=pl.ANY)
scalars = pl.BlockSpec(memory_space=pltpu.SMEM)
in_vmem = pl.BlockSpec(memory_space=pltpu.VMEM)


def split_parts(count, rows, depth):
    tiles, half = count // tile, rows // 2
    out = [jax.ShapeDtypeStruct((half, count), bf16)] * 2
    scratch = [
        pltpu.VMEM((rows, depth), bf16),
        pltpu.VMEM((half, count), bf16),
        pltpu.VMEM((half, count), bf16),
        pltpu.SemaphoreType.DMA((tiles + 1,)),
        pltpu.SemaphoreType.DMA((2,)),
    ]
    return out, scratch


def split_product(rows, weight, dim, place):
    out, scratch = split_parts(weight.shape[1 - dim], *rows.shape)
    return pl.pallas_call(
        functools.partial(split_kernel, dim),
        in_specs=[scalars, anywhere, anywhere],
        out_specs=[anywhere, anywhere],
        out_shape=out,
        scratch_shapes=scratch + [pltpu.VMEM(held_shape(weight, dim), bf16)],
        compiler_params=params,
        cost_estimate=cost,
    )(place, rows, weight)


def enter_product(spot, slot, up, down, tok, place):
    out, scratch = split_parts(up.shape[1], spot.shape[0], slot.shape[1])
    return pl.pallas_call(
        enter_kernel,
        in_specs=[scalars, in_vmem, anywhere, anywhere, anywhere],
        out_specs=[anywhere, anywhere, in_vmem],
        out_shape=out + [jax.ShapeDtypeStruct((2 * tok, slot.shape[1]), bf16)],
        scratch_shapes=scratch
        + [
            pltpu.VMEM(held_shape(up, 0), bf16),
            pltpu.VMEM(held_shape(down, 1), bf16),
            pltpu.VMEM(slot.shape, bf16),
        ],
        compiler_params=params,
        cost_estimate=cost,
    )(place, spot, slot, up, down)


def rank_kernel(table_rows, place, row_ids, column_ids, spot, wanted, most):
    count, capacity = spot.shape[0], wanted.shape[0]
    shift = table_rows.bit_length() - 1
    across_ids, down_ids = row_ids[...], column_ids[...]
    here = lax.broadcasted_iota(jnp.int32, (count, count), 0)
    there = lax.broadcasted_iota(jnp.int32, (count, count), 1)
    equal = across_ids == down_ids
    same = (across_ids >> shift) == (down_ids >> shift)

    def ones(mask):
        return jnp.where(mask, 1.0, 0.0)

    repeat_down = jnp.sum(ones(equal & (there < here)), axis=1, keepdims=True)
    repeat_across = jnp.sum(ones(equal & (here < there)), axis=0, keepdims=True)
    number = jnp.sum(
        ones(same & (here < there) & (repeat_down == 0.0)), axis=0, keepdims=True
    )
    mine = jnp.sum(
        jnp.where(equal & (repeat_across == 0.0), number, 0.0), axis=1, keepdims=True
    )
    spot[...] = (down_ids >> shift) * capacity + mine.astype(jnp.int32)
    slot = lax.broadcasted_iota(jnp.int32, (capacity, count), 0)
    local = across_ids - (place[2] << shift)
    named = (
        (local >= 0)
        & (local < table_rows)
        & (repeat_across == 0.0)
        & (number.astype(jnp.int32) == slot)
    )
    wanted[...] = (
        jnp.sum(jnp.where(named, local.astype(f32) + 1.0, 0.0), axis=1, keepdims=True) - 1.0
    ).astype(jnp.int32)
    most[...] = jnp.max(mine, axis=0, keepdims=True).astype(jnp.int32) + 1


def rank(ids, table_rows, capacity, place):
    count = ids.shape[0]
    return pl.pallas_call(
        functools.partial(rank_kernel, table_rows),
        in_specs=[scalars, in_vmem, in_vmem],
        out_specs=[in_vmem] * 3,
        out_shape=[
            jax.ShapeDtypeStruct((count, 1), jnp.int32),
            jax.ShapeDtypeStruct((capacity, 1), jnp.int32),
            jax.ShapeDtypeStruct((1, 1), jnp.int32),
        ],
        compiler_params=params,
        cost_estimate=cost,
    )(place, ids[None, :], ids[:, None])


def join_kernel(dim, swapped, place, mine, other, weight, *refs):
    if swapped:
        instead, refs = refs[0], refs[1:]
    out, rows, staged, arrived, left, held = refs
    half = mine.shape[0]
    tiles = held.shape[0]

    def run():
        parts = [
            pltpu.make_async_copy(
                part,
                rows.at[pl.ds(pl.multiple_of(position * half, half), half)],
                arrived.at[tiles + index],
            )
            for index, (part, position) in enumerate(((mine, place[0]), (other, 1 - place[0])))
        ]
        for copy in parts:
            copy.start()
        copies = start_weight(weight, dim, held, arrived)
        for copy in parts:
            copy.wait()
        for index, copy in enumerate(copies):
            copy.wait()
            columns = slice(index * tile, (index + 1) * tile)
            staged[:, columns] = multiply(rows[...], held[index], dim).astype(bf16)
        done = pltpu.make_async_copy(staged, out, left.at[0])
        done.start()
        done.wait()

    if swapped:
        pl.when(place[1] == 0)(run)

        @pl.when(place[1] != 0)
        def _():
            copy = pltpu.make_async_copy(instead, out, left.at[0])
            copy.start()
            copy.wait()

    else:
        run()


def join_product(mine, other, weight, dim, place, instead=()):
    count = weight.shape[1 - dim]
    tiles = count // tile
    half, depth = mine.shape
    return pl.pallas_call(
        functools.partial(join_kernel, dim, bool(instead)),
        in_specs=[scalars] + [anywhere] * (3 + len(instead)),
        out_specs=anywhere,
        out_shape=jax.ShapeDtypeStruct((2 * half, count), bf16),
        scratch_shapes=[
            pltpu.VMEM((2 * half, depth), bf16),
            pltpu.VMEM((2 * half, count), bf16),
            pltpu.SemaphoreType.DMA((tiles + 2,)),
            pltpu.SemaphoreType.DMA((1,)),
            pltpu.VMEM(held_shape(weight, dim), bf16),
        ],
        compiler_params=params,
        cost_estimate=cost,
    )(place, mine, other, weight, *instead)


def lookup_kernel(wanted, table, out, chosen):
    @pl.when(pl.program_id(0) == 0)
    def _():
        row = lax.broadcasted_iota(jnp.int32, chosen.shape, 1)
        chosen[...] = jnp.where(row == wanted[...], 1.0, 0.0).astype(bf16)

    out[...] = multiply(chosen[...], table[...], 0).astype(bf16)


def lookup(wanted, table):
    count = wanted.shape[0]
    rows, feat = table.shape
    return pl.pallas_call(
        lookup_kernel,
        grid=(feat // tile,),
        in_specs=[
            pl.BlockSpec(wanted.shape, lambda i: (0, 0)),
            pl.BlockSpec((rows, tile), lambda i: (0, i)),
        ],
        out_specs=pl.BlockSpec((count, tile), lambda i: (0, i)),
        scratch_shapes=[pltpu.VMEM((count, rows), bf16)],
        out_shape=jax.ShapeDtypeStruct((count, feat), bf16),
        compiler_params=params,
        cost_estimate=cost,
    )(wanted, table)


def tie(*values):
    return lax.optimization_barrier(values)


def after(value, *earlier):
    return lax.optimization_barrier((value, *earlier))[0]


def on_device(token_ids, table, w_up, w_down, cotangent):
    micro, tok, feat = cotangent.shape
    dp = lax.axis_size("dp")
    up = w_up[0]
    down = w_down[0]
    is_first = lax.axis_index("segment") == 0
    here = lax.axis_index("dp")
    place = jnp.stack(
        [lax.axis_index("mp") % 2, lax.axis_index("segment"), here]
    ).astype(jnp.int32)
    capacity = micro * tok
    table_rows = table.shape[0]
    own_cot = cotangent.reshape(capacity, feat)

    def whole(slot):
        return slot.reshape(-1, feat)

    def blocks(rows):
        return rows.reshape(dp, -1, feat)

    def either(left, right):
        return jnp.where(is_first, left, right)

    def chip_sum(kept, sent):
        return (kept.astype(f32) + swap(sent, 1).astype(f32)).astype(bf16)

    def finish(chip, came):
        return chip.astype(f32) + came.astype(f32)

    def active(summed):
        return gelu_value(summed.astype(f32)).astype(bf16)

    def slope(saved, summed):
        return (gelu_slope(saved) * summed.astype(f32)).astype(bf16)

    spot, wanted, most = rank(token_ids.reshape(-1), table_rows, capacity, place)
    fits = most[0, 0] <= capacity

    def sparse():
        return lookup(wanted, table)

    def dense():
        by_owner = token_ids.reshape(micro, dp, tok).transpose(1, 0, 2).reshape(-1, 1)
        fetched = lookup(by_owner - here * table_rows, table)
        return collect(exchange(blocks(fetched))).astype(bf16)

    found = lax.cond(fits, sparse, dense)
    slot_2 = whole(exchange(spread(either(found, own_cot))))
    token = jnp.arange(micro * dp * tok, dtype=jnp.int32)
    in_order = (token // tok % dp) * capacity + token // (dp * tok) * tok + token % tok
    spot = jnp.where(is_first & fits, spot, in_order[:, None])
    spot = spot.reshape(micro, 2, -1).transpose(1, 0, 2).reshape(-1, 1)

    kept, sent, embedded = enter_product(spot, slot_2, up, down, tok, place)
    chip = chip_sum(kept, sent)
    half = chip.shape[0] // 2
    emb_a, emb_b = embedded[:tok], embedded[tok:]
    came_a, came_b = swap(chip[:half], 2), swap(chip[half:], 2)
    first_a = finish(chip[:half], came_a)
    hid_a, first_a = active(first_a), first_a.astype(bf16)
    mix_a = join_product(hid_a, swap(hid_a, 1), down, 0, place)
    slot_4 = exchange(blocks(mix_a))
    first_b = finish(chip[half:], after(came_b, mix_a))
    hid_b, first_b = active(first_b), first_b.astype(bf16)
    act0_a = plus(emb_a, after(slot_4, hid_b))
    pass_a = across(act0_a)
    hid_b = after(hid_b, act0_a)
    mix_b = join_product(hid_b, swap(hid_b, 1), down, 0, place)

    slot_5 = exchange(after(either(blocks(mix_b), spread(pass_a)), slot_4))
    slope_a = gelu_slope(after(first_a, mix_b).astype(f32)).astype(bf16)
    slope_b = gelu_slope(after(first_b, mix_b).astype(f32)).astype(bf16)
    slot_5 = after(slot_5, slope_a, slope_b)
    act0_b = plus(emb_b, slot_5)
    pass_b = across(act0_b)
    kept_a, sent_a = split_product(whole(after(slot_5, act0_b)), up, 0, place)
    pass_b, kept_a, sent_a = tie(pass_b, kept_a, sent_a)
    chip_a = chip_sum(kept_a, sent_a)
    came_a = swap(chip_a, 2)
    slot_6 = exchange(after(spread(after(pass_b, kept_a)), slot_5))
    pre_a = finish(chip_a, came_a)
    back_a = slope(pre_a, first_a)
    pre_a = pre_a.astype(bf16)
    mix_a = join_product(back_a, swap(back_a, 1), up, 1, place)
    kept_b, sent_b = split_product(whole(after(slot_6, mix_a)), up, 0, place)
    slot_7 = exchange(after(blocks(mix_a), slot_6))
    chip_b = chip_sum(kept_b, sent_b)
    came_b = swap(chip_b, 2)
    hid_a = active(after(pre_a, chip_b))
    out_a = join_product(hid_a, swap(hid_a, 1), down, 0, place)
    grad1_a = plus(cotangent[0], after(slot_7, out_a))
    gone_a = across(grad1_a)
    pre_b = finish(chip_b, after(came_b, grad1_a))
    back_b = slope(pre_b, first_b)
    pre_b = pre_b.astype(bf16)
    mix_b = join_product(back_b, swap(back_b, 1), up, 1, place)
    slot_8 = exchange(
        after(either(spread(after(gone_a, mix_b)), blocks(mix_b)), slot_7)
    )
    hid_b = active(after(pre_b, mix_b))
    out_b = join_product(hid_b, swap(hid_b, 1), down, 0, place)
    slot_8 = after(slot_8, out_b)

    grad1_b = plus(cotangent[1], slot_8)
    gone_b = across(grad1_b)
    kept_a, sent_a = split_product(whole(after(slot_8, grad1_b)), down, 1, place)
    send_9 = either(spread(gone_b), blocks(out_a))
    send_9, kept_a, sent_a = tie(send_9, kept_a, sent_a)
    slot_9 = exchange(after(send_9, slot_8))
    chip_a = chip_sum(kept_a, sent_a)
    came_a = swap(chip_a, 2)
    back_a = (slope_a.astype(f32) * finish(chip_a, came_a)).astype(bf16)
    far_a = swap(back_a, 1)
    kept_b, sent_b = split_product(whole(after(slot_9, far_a)), down, 1, place)
    mix_a = join_product(after(back_a, kept_b), far_a, up, 1, place, (out_b,))
    chip_b = chip_sum(after(kept_b, mix_a), sent_b)
    came_b = swap(chip_b, 2)
    slot_10 = exchange(after(blocks(mix_a), slot_9))
    back_b = (slope_b.astype(f32) * finish(chip_b, after(came_b, mix_a))).astype(bf16)
    mix_b = join_product(back_b, swap(back_b, 1), up, 1, place)
    slot_10 = after(slot_10, mix_b)
    slot_11 = exchange(after(blocks(mix_b), slot_10))
    act1_a = plus(pass_a, after(slot_9, mix_b))
    act1_b = plus(pass_b, slot_10)
    grad0_a = plus(gone_a, slot_10)
    grad0_b = plus(gone_b, after(slot_11, act1_a, act1_b, grad0_a))

    acts = jnp.stack([either(act0_a, act1_a), either(act0_b, act1_b)])
    grads = jnp.stack([either(grad0_a, grad1_a), either(grad0_b, grad1_b)])
    return (acts[None], grads[None])


def solution(mesh):
    return jax.shard_map(
        on_device,
        mesh=mesh,
        in_specs=(
            P(),
            P("dp", "mp"),
            P("segment", "mp", "dp"),
            P("segment", "dp", "mp"),
            P(None, "dp", "mp"),
        ),
        out_specs=(P("segment", None, "dp", "mp"), P("segment", None, "dp", "mp")),
        check_vma=False,
    )
```

```python
import functools

import jax
import jax.numpy as jnp
from jax import lax
from jax.experimental import pallas as pl
from jax.experimental.pallas import tpu as pltpu
from jax.sharding import PartitionSpec as P

root_coef = 0.7978845608028654
bf16, f32 = jnp.bfloat16, jnp.float32
tile = 512
cost = pl.CostEstimate(flops=200_000_000, bytes_accessed=1_000_000, transcendentals=0)
params = pltpu.CompilerParams(vmem_limit_bytes=44 * 1024 * 1024)


def gelu_value(value):
    return 0.5 * value * (1.0 + jnp.tanh(root_coef * (value + 0.044715 * value * value * value)))


def gelu_slope(value):
    inner = jnp.tanh(root_coef * (value + 0.044715 * value * value * value))
    return 0.5 * (1.0 + inner) + 0.5 * value * (1.0 - inner * inner) * root_coef * (
        1.0 + 0.134145 * value * value
    )


def swap(value, bit):
    return lax.ppermute(value, "mp", [(i, i ^ bit) for i in range(4)])


def across(value):
    return lax.ppermute(value, "segment", [(0, 1), (1, 0)])


def exchange(blocks):
    return lax.all_to_all(blocks, "dp", 0, 0)


def spread(own):
    return jnp.broadcast_to(own[None], (lax.axis_size("dp"),) + own.shape)


def collect(blocks):
    return jnp.sum(blocks.astype(f32), axis=0)


def plus(own, blocks):
    return (own.astype(f32) + collect(blocks)).astype(bf16)


def multiply(rows, weight, dim):
    return lax.dot_general(
        rows, weight, (((1,), (dim,)), ((), ())), preferred_element_type=f32
    )


def start_weight(weight, dim, held, arrived):
    copies = []
    for index in range(held.shape[0]):
        columns = pl.ds(index * tile, tile)
        source = weight.at[:, columns] if dim == 0 else weight.at[columns, :]
        copies.append(pltpu.make_async_copy(source, held.at[index], arrived.at[index]))
        copies[-1].start()
    return copies


def split_tiles(rows, copies, held, dim, low, staged_kept, staged_sent, kept, sent, left):
    half = kept.shape[0]
    pending = []
    for index, copy in enumerate(copies):
        copy.wait()
        total = multiply(rows[...], held[index], dim)
        staged_kept[index] = jnp.where(low, total[:half], total[half:]).astype(bf16)
        staged_sent[index] = jnp.where(low, total[half:], total[:half]).astype(bf16)
        columns = pl.ds(index * tile, tile)
        pending += [
            pltpu.make_async_copy(staged_sent.at[index], sent.at[:, columns], left.at[2 * index]),
            pltpu.make_async_copy(
                staged_kept.at[index], kept.at[:, columns], left.at[2 * index + 1]
            ),
        ]
        pending[-2].start()
        pending[-1].start()
    for copy in pending:
        copy.wait()


def held_shape(weight, dim):
    depth, count = weight.shape[dim], weight.shape[1 - dim]
    return (count // tile, depth, tile) if dim == 0 else (count // tile, tile, depth)


def split_kernel(dim, place, rows_in, weight, kept, sent, rows, *refs):
    staged_kept, staged_sent, arrived, left, held = refs
    rows_copy = pltpu.make_async_copy(rows_in, rows, arrived.at[arrived.shape[0] - 1])
    rows_copy.start()
    copies = start_weight(weight, dim, held, arrived)
    rows_copy.wait()
    low = place[0] == 0
    split_tiles(rows, copies, held, dim, low, staged_kept, staged_sent, kept, sent, left)


def enter_kernel(place, spot, slot_in, up, down, kept, sent, own, rows, *refs):
    staged_kept, staged_sent, arrived, left, held_up, held_down, slot = refs
    slot_copy = pltpu.make_async_copy(slot_in, slot, arrived.at[arrived.shape[0] - 1])
    slot_copy.start()
    low = place[0] == 0
    tok = own.shape[0] // 2

    def run(weight, dim, held):
        copies = start_weight(weight, dim, held, arrived)
        index = lax.broadcasted_iota(jnp.int32, (rows.shape[0], slot.shape[0]), 1)
        chosen = jnp.where(index == spot[...], 1.0, 0.0).astype(bf16)
        slot_copy.wait()
        rows[...] = multiply(chosen, slot[...], 0).astype(bf16)
        quarter = rows.shape[0] // 4
        first = place[2] * tok
        first = first + jnp.where(first >= quarter, quarter, 0)
        for m in range(2):
            begin = pl.multiple_of(first + m * quarter, tok)
            own[m * tok : (m + 1) * tok] = rows[pl.ds(begin, tok)]
        split_tiles(rows, copies, held, dim, low, staged_kept, staged_sent, kept, sent, left)

    @pl.when(place[1] == 0)
    def _():
        run(up, 0, held_up)

    @pl.when(place[1] != 0)
    def _():
        run(down, 1, held_down)


anywhere = pl.BlockSpec(memory_space=pl.ANY)
scalars = pl.BlockSpec(memory_space=pltpu.SMEM)
in_vmem = pl.BlockSpec(memory_space=pltpu.VMEM)


def split_parts(count, rows, depth):
    tiles, half = count // tile, rows // 2
    out = [jax.ShapeDtypeStruct((half, count), bf16)] * 2
    scratch = [
        pltpu.VMEM((rows, depth), bf16),
        pltpu.VMEM((tiles, half, tile), bf16),
        pltpu.VMEM((tiles, half, tile), bf16),
        pltpu.SemaphoreType.DMA((tiles + 1,)),
        pltpu.SemaphoreType.DMA((2 * tiles,)),
    ]
    return out, scratch


def split_product(rows, weight, dim, place):
    out, scratch = split_parts(weight.shape[1 - dim], *rows.shape)
    return pl.pallas_call(
        functools.partial(split_kernel, dim),
        in_specs=[scalars, anywhere, anywhere],
        out_specs=[anywhere, anywhere],
        out_shape=out,
        scratch_shapes=scratch + [pltpu.VMEM(held_shape(weight, dim), bf16)],
        compiler_params=params,
        cost_estimate=cost,
    )(place, rows, weight)


def enter_product(spot, slot, up, down, tok, place):
    out, scratch = split_parts(up.shape[1], spot.shape[0], slot.shape[1])
    return pl.pallas_call(
        enter_kernel,
        in_specs=[scalars, in_vmem, anywhere, anywhere, anywhere],
        out_specs=[anywhere, anywhere, in_vmem],
        out_shape=out + [jax.ShapeDtypeStruct((2 * tok, slot.shape[1]), bf16)],
        scratch_shapes=scratch
        + [
            pltpu.VMEM(held_shape(up, 0), bf16),
            pltpu.VMEM(held_shape(down, 1), bf16),
            pltpu.VMEM(slot.shape, bf16),
        ],
        compiler_params=params,
        cost_estimate=cost,
    )(place, spot, slot, up, down)


def rank_kernel(table_rows, place, row_ids, column_ids, spot, wanted, most):
    count, capacity = spot.shape[0], wanted.shape[0]
    shift = table_rows.bit_length() - 1
    across_ids, down_ids = row_ids[...], column_ids[...]
    here = lax.broadcasted_iota(jnp.int32, (count, count), 0)
    there = lax.broadcasted_iota(jnp.int32, (count, count), 1)
    equal = across_ids == down_ids
    same = (across_ids >> shift) == (down_ids >> shift)

    def ones(mask):
        return jnp.where(mask, 1.0, 0.0)

    repeat_down = jnp.sum(ones(equal & (there < here)), axis=1, keepdims=True)
    repeat_across = jnp.sum(ones(equal & (here < there)), axis=0, keepdims=True)
    number = jnp.sum(
        ones(same & (here < there) & (repeat_down == 0.0)), axis=0, keepdims=True
    )
    mine = jnp.sum(
        jnp.where(equal & (repeat_across == 0.0), number, 0.0), axis=1, keepdims=True
    )
    spot[...] = (down_ids >> shift) * capacity + mine.astype(jnp.int32)
    slot = lax.broadcasted_iota(jnp.int32, (capacity, count), 0)
    local = across_ids - (place[2] << shift)
    named = (
        (local >= 0)
        & (local < table_rows)
        & (repeat_across == 0.0)
        & (number.astype(jnp.int32) == slot)
    )
    wanted[...] = (
        jnp.sum(jnp.where(named, local.astype(f32) + 1.0, 0.0), axis=1, keepdims=True) - 1.0
    ).astype(jnp.int32)
    most[...] = jnp.max(mine, axis=0, keepdims=True).astype(jnp.int32) + 1


def rank(ids, table_rows, capacity, place):
    count = ids.shape[0]
    return pl.pallas_call(
        functools.partial(rank_kernel, table_rows),
        in_specs=[scalars, in_vmem, in_vmem],
        out_specs=[in_vmem] * 3,
        out_shape=[
            jax.ShapeDtypeStruct((count, 1), jnp.int32),
            jax.ShapeDtypeStruct((capacity, 1), jnp.int32),
            jax.ShapeDtypeStruct((1, 1), jnp.int32),
        ],
        compiler_params=params,
        cost_estimate=cost,
    )(place, ids[None, :], ids[:, None])


def join_kernel(dim, swapped, place, mine, other, weight, *refs):
    if swapped:
        instead, refs = refs[0], refs[1:]
    out, rows, staged, arrived, left, held = refs
    half = mine.shape[0]
    tiles = held.shape[0]

    def run():
        parts = [
            pltpu.make_async_copy(
                part,
                rows.at[pl.ds(pl.multiple_of(position * half, half), half)],
                arrived.at[tiles + index],
            )
            for index, (part, position) in enumerate(((mine, place[0]), (other, 1 - place[0])))
        ]
        for copy in parts:
            copy.start()
        copies = start_weight(weight, dim, held, arrived)
        for copy in parts:
            copy.wait()
        pending = []
        for index, copy in enumerate(copies):
            copy.wait()
            staged[index] = multiply(rows[...], held[index], dim).astype(bf16)
            pending.append(
                pltpu.make_async_copy(
                    staged.at[index], out.at[:, pl.ds(index * tile, tile)], left.at[index]
                )
            )
            pending[-1].start()
        for copy in pending:
            copy.wait()

    if swapped:
        pl.when(place[1] == 0)(run)

        @pl.when(place[1] != 0)
        def _():
            copy = pltpu.make_async_copy(instead, out, left.at[0])
            copy.start()
            copy.wait()

    else:
        run()


def join_product(mine, other, weight, dim, place, instead=()):
    count = weight.shape[1 - dim]
    tiles = count // tile
    half, depth = mine.shape
    return pl.pallas_call(
        functools.partial(join_kernel, dim, bool(instead)),
        in_specs=[scalars] + [anywhere] * (3 + len(instead)),
        out_specs=anywhere,
        out_shape=jax.ShapeDtypeStruct((2 * half, count), bf16),
        scratch_shapes=[
            pltpu.VMEM((2 * half, depth), bf16),
            pltpu.VMEM((tiles, 2 * half, tile), bf16),
            pltpu.SemaphoreType.DMA((tiles + 2,)),
            pltpu.SemaphoreType.DMA((tiles,)),
            pltpu.VMEM(held_shape(weight, dim), bf16),
        ],
        compiler_params=params,
        cost_estimate=cost,
    )(place, mine, other, weight, *instead)


def lookup_kernel(wanted, table, out, chosen):
    @pl.when(pl.program_id(0) == 0)
    def _():
        row = lax.broadcasted_iota(jnp.int32, chosen.shape, 1)
        chosen[...] = jnp.where(row == wanted[...], 1.0, 0.0).astype(bf16)

    out[...] = multiply(chosen[...], table[...], 0).astype(bf16)


def lookup(wanted, table):
    count = wanted.shape[0]
    rows, feat = table.shape
    return pl.pallas_call(
        lookup_kernel,
        grid=(feat // tile,),
        in_specs=[
            pl.BlockSpec(wanted.shape, lambda i: (0, 0)),
            pl.BlockSpec((rows, tile), lambda i: (0, i)),
        ],
        out_specs=pl.BlockSpec((count, tile), lambda i: (0, i)),
        scratch_shapes=[pltpu.VMEM((count, rows), bf16)],
        out_shape=jax.ShapeDtypeStruct((count, feat), bf16),
        compiler_params=params,
        cost_estimate=cost,
    )(wanted, table)


def tie(*values):
    return lax.optimization_barrier(values)


def after(value, *earlier):
    return lax.optimization_barrier((value, *earlier))[0]


def on_device(token_ids, table, w_up, w_down, cotangent):
    micro, tok, feat = cotangent.shape
    dp = lax.axis_size("dp")
    up = w_up[0]
    down = w_down[0]
    is_first = lax.axis_index("segment") == 0
    here = lax.axis_index("dp")
    place = jnp.stack(
        [lax.axis_index("mp") % 2, lax.axis_index("segment"), here]
    ).astype(jnp.int32)
    capacity = micro * tok
    table_rows = table.shape[0]
    own_cot = cotangent.reshape(capacity, feat)

    def whole(slot):
        return slot.reshape(-1, feat)

    def blocks(rows):
        return rows.reshape(dp, -1, feat)

    def either(left, right):
        return jnp.where(is_first, left, right)

    def chip_sum(kept, sent):
        return (kept.astype(f32) + swap(sent, 1).astype(f32)).astype(bf16)

    def finish(chip, came):
        return chip.astype(f32) + came.astype(f32)

    def active(summed):
        return gelu_value(summed.astype(f32)).astype(bf16)

    def slope(saved, summed):
        return (gelu_slope(saved) * summed.astype(f32)).astype(bf16)

    spot, wanted, most = rank(token_ids.reshape(-1), table_rows, capacity, place)
    fits = most[0, 0] <= capacity

    def sparse():
        return lookup(wanted, table)

    def dense():
        by_owner = token_ids.reshape(micro, dp, tok).transpose(1, 0, 2).reshape(-1, 1)
        fetched = lookup(by_owner - here * table_rows, table)
        return collect(exchange(blocks(fetched))).astype(bf16)

    found = lax.cond(fits, sparse, dense)
    slot_2 = whole(exchange(spread(either(found, own_cot))))
    token = jnp.arange(micro * dp * tok, dtype=jnp.int32)
    in_order = (token // tok % dp) * capacity + token // (dp * tok) * tok + token % tok
    spot = jnp.where(is_first & fits, spot, in_order[:, None])
    spot = spot.reshape(micro, 2, -1).transpose(1, 0, 2).reshape(-1, 1)

    kept, sent, embedded = enter_product(spot, slot_2, up, down, tok, place)
    chip = chip_sum(kept, sent)
    half = chip.shape[0] // 2
    emb_a, emb_b = embedded[:tok], embedded[tok:]
    came_a, came_b = swap(chip[:half], 2), swap(chip[half:], 2)
    first_a = finish(chip[:half], came_a)
    hid_a, first_a = active(first_a), first_a.astype(bf16)
    mix_a = join_product(hid_a, swap(hid_a, 1), down, 0, place)
    slot_4 = exchange(blocks(mix_a))
    first_b = finish(chip[half:], after(came_b, mix_a))
    hid_b, first_b = active(first_b), first_b.astype(bf16)
    mix_b = join_product(hid_b, swap(hid_b, 1), down, 0, place)
    act0_a = plus(emb_a, after(slot_4, mix_b))
    pass_a = across(act0_a)

    slot_5 = exchange(after(either(blocks(mix_b), spread(pass_a)), slot_4))
    slope_a = gelu_slope(after(first_a, mix_b).astype(f32)).astype(bf16)
    slope_b = gelu_slope(after(first_b, mix_b).astype(f32)).astype(bf16)
    slot_5 = after(slot_5, slope_a, slope_b)
    act0_b = plus(emb_b, slot_5)
    pass_b = across(act0_b)
    kept_a, sent_a = split_product(whole(after(slot_5, act0_b)), up, 0, place)
    pass_b, kept_a, sent_a = tie(pass_b, kept_a, sent_a)
    chip_a = chip_sum(kept_a, sent_a)
    came_a = swap(chip_a, 2)
    slot_6 = exchange(after(spread(after(pass_b, kept_a)), slot_5))
    pre_a = finish(chip_a, came_a)
    back_a = slope(pre_a, first_a)
    pre_a = pre_a.astype(bf16)
    mix_a = join_product(back_a, swap(back_a, 1), up, 1, place)
    kept_b, sent_b = split_product(whole(after(slot_6, mix_a)), up, 0, place)
    slot_7 = exchange(after(blocks(mix_a), slot_6))
    chip_b = chip_sum(kept_b, sent_b)
    came_b = swap(chip_b, 2)
    hid_a = active(after(pre_a, chip_b))
    out_a = join_product(hid_a, swap(hid_a, 1), down, 0, place)
    grad1_a = plus(cotangent[0], after(slot_7, out_a))
    gone_a = across(grad1_a)
    pre_b = finish(chip_b, after(came_b, grad1_a))
    back_b = slope(pre_b, first_b)
    pre_b = pre_b.astype(bf16)
    mix_b = join_product(back_b, swap(back_b, 1), up, 1, place)
    slot_8 = exchange(
        after(either(spread(after(gone_a, mix_b)), blocks(mix_b)), slot_7)
    )
    hid_b = active(after(pre_b, mix_b))
    out_b = join_product(hid_b, swap(hid_b, 1), down, 0, place)
    slot_8 = after(slot_8, out_b)

    grad1_b = plus(cotangent[1], slot_8)
    gone_b = across(grad1_b)
    kept_a, sent_a = split_product(whole(after(slot_8, grad1_b)), down, 1, place)
    send_9 = either(spread(gone_b), blocks(out_a))
    send_9, kept_a, sent_a = tie(send_9, kept_a, sent_a)
    slot_9 = exchange(after(send_9, slot_8))
    chip_a = chip_sum(kept_a, sent_a)
    came_a = swap(chip_a, 2)
    kept_b, sent_b = split_product(whole(slot_9), down, 1, place)
    back_a = (slope_a.astype(f32) * finish(chip_a, after(came_a, kept_b))).astype(bf16)
    far_a = swap(back_a, 1)
    chip_b = chip_sum(kept_b, sent_b)
    came_b = swap(chip_b, 2)
    mix_a = join_product(after(back_a, chip_b), far_a, up, 1, place, (out_b,))
    slot_10 = exchange(after(blocks(mix_a), slot_9))
    act1_a = plus(pass_a, after(slot_9, mix_a))
    back_b = (slope_b.astype(f32) * finish(chip_b, after(came_b, act1_a))).astype(bf16)
    mix_b = join_product(back_b, swap(back_b, 1), up, 1, place)
    slot_11 = exchange(after(blocks(mix_b), slot_10))
    act1_b = plus(pass_b, slot_10)
    grad0_a = plus(gone_a, slot_10)
    grad0_b = plus(gone_b, after(slot_11, act1_b, grad0_a))

    acts = jnp.stack([either(act0_a, act1_a), either(act0_b, act1_b)])
    grads = jnp.stack([either(grad0_a, grad1_a), either(grad0_b, grad1_b)])
    return (acts[None], grads[None])


def solution(mesh):
    return jax.shard_map(
        on_device,
        mesh=mesh,
        in_specs=(
            P(),
            P("dp", "mp"),
            P("segment", "mp", "dp"),
            P("segment", "dp", "mp"),
            P(None, "dp", "mp"),
        ),
        out_specs=(P("segment", None, "dp", "mp"), P("segment", None, "dp", "mp")),
        check_vma=False,
    )
```

```python
import functools

import jax
import jax.numpy as jnp
from jax import lax
from jax.experimental import pallas as pl
from jax.experimental.pallas import tpu as pltpu
from jax.sharding import PartitionSpec as P

root_coef = 0.7978845608028654
bf16, f32 = jnp.bfloat16, jnp.float32
tile = 512
cost = pl.CostEstimate(flops=200_000_000, bytes_accessed=1_000_000, transcendentals=0)
params = pltpu.CompilerParams(vmem_limit_bytes=44 * 1024 * 1024)


def gelu_value(value):
    return 0.5 * value * (1.0 + jnp.tanh(root_coef * (value + 0.044715 * value * value * value)))


def gelu_slope(value):
    inner = jnp.tanh(root_coef * (value + 0.044715 * value * value * value))
    return 0.5 * (1.0 + inner) + 0.5 * value * (1.0 - inner * inner) * root_coef * (
        1.0 + 0.134145 * value * value
    )


def swap(value, bit):
    return lax.ppermute(value, "mp", [(i, i ^ bit) for i in range(4)])


def across(value):
    return lax.ppermute(value, "segment", [(0, 1), (1, 0)])


def exchange(blocks):
    return lax.all_to_all(blocks, "dp", 0, 0)


def spread(own):
    return jnp.broadcast_to(own[None], (lax.axis_size("dp"),) + own.shape)


def collect(blocks):
    return jnp.sum(blocks.astype(f32), axis=0)


def plus(own, blocks):
    return (own.astype(f32) + collect(blocks)).astype(bf16)


def multiply(rows, weight, dim):
    return lax.dot_general(
        rows, weight, (((1,), (dim,)), ((), ())), preferred_element_type=f32
    )


def start_weight(weight, dim, held, arrived):
    copies = []
    for index in range(held.shape[0]):
        columns = pl.ds(index * tile, tile)
        source = weight.at[:, columns] if dim == 0 else weight.at[columns, :]
        copies.append(pltpu.make_async_copy(source, held.at[index], arrived.at[index]))
        copies[-1].start()
    return copies


def split_tiles(rows, copies, held, dim, low, staged_kept, staged_sent, kept, sent, left):
    half = kept.shape[0]
    for index, copy in enumerate(copies):
        copy.wait()
        total = multiply(rows[...], held[index], dim)
        columns = slice(index * tile, (index + 1) * tile)
        staged_kept[:, columns] = jnp.where(low, total[:half], total[half:]).astype(bf16)
        staged_sent[:, columns] = jnp.where(low, total[half:], total[:half]).astype(bf16)
    pending = [
        pltpu.make_async_copy(staged_sent, sent, left.at[0]),
        pltpu.make_async_copy(staged_kept, kept, left.at[1]),
    ]
    for copy in pending:
        copy.start()
    for copy in pending:
        copy.wait()


def held_shape(weight, dim):
    depth, count = weight.shape[dim], weight.shape[1 - dim]
    return (count // tile, depth, tile) if dim == 0 else (count // tile, tile, depth)


def split_kernel(dim, place, rows_in, weight, kept, sent, rows, *refs):
    staged_kept, staged_sent, arrived, left, held = refs
    rows_copy = pltpu.make_async_copy(rows_in, rows, arrived.at[arrived.shape[0] - 1])
    rows_copy.start()
    copies = start_weight(weight, dim, held, arrived)
    rows_copy.wait()
    low = place[0] == 0
    split_tiles(rows, copies, held, dim, low, staged_kept, staged_sent, kept, sent, left)


def enter_kernel(place, spot, slot_in, up, down, kept, sent, own, rows, *refs):
    staged_kept, staged_sent, arrived, left, held_up, held_down, slot = refs
    slot_copy = pltpu.make_async_copy(slot_in, slot, arrived.at[arrived.shape[0] - 1])
    slot_copy.start()
    low = place[0] == 0
    tok = own.shape[0] // 2

    def run(weight, dim, held):
        copies = start_weight(weight, dim, held, arrived)
        index = lax.broadcasted_iota(jnp.int32, (rows.shape[0], slot.shape[0]), 1)
        chosen = jnp.where(index == spot[...], 1.0, 0.0).astype(bf16)
        slot_copy.wait()
        rows[...] = multiply(chosen, slot[...], 0).astype(bf16)
        quarter = rows.shape[0] // 4
        first = place[2] * tok
        first = first + jnp.where(first >= quarter, quarter, 0)
        for m in range(2):
            begin = pl.multiple_of(first + m * quarter, tok)
            own[m * tok : (m + 1) * tok] = rows[pl.ds(begin, tok)]
        split_tiles(rows, copies, held, dim, low, staged_kept, staged_sent, kept, sent, left)

    @pl.when(place[1] == 0)
    def _():
        run(up, 0, held_up)

    @pl.when(place[1] != 0)
    def _():
        run(down, 1, held_down)


anywhere = pl.BlockSpec(memory_space=pl.ANY)
scalars = pl.BlockSpec(memory_space=pltpu.SMEM)
in_vmem = pl.BlockSpec(memory_space=pltpu.VMEM)


def split_parts(count, rows, depth):
    tiles, half = count // tile, rows // 2
    out = [jax.ShapeDtypeStruct((half, count), bf16)] * 2
    scratch = [
        pltpu.VMEM((rows, depth), bf16),
        pltpu.VMEM((half, count), bf16),
        pltpu.VMEM((half, count), bf16),
        pltpu.SemaphoreType.DMA((tiles + 1,)),
        pltpu.SemaphoreType.DMA((2,)),
    ]
    return out, scratch


def split_product(rows, weight, dim, place):
    out, scratch = split_parts(weight.shape[1 - dim], *rows.shape)
    return pl.pallas_call(
        functools.partial(split_kernel, dim),
        in_specs=[scalars, anywhere, anywhere],
        out_specs=[anywhere, anywhere],
        out_shape=out,
        scratch_shapes=scratch + [pltpu.VMEM(held_shape(weight, dim), bf16)],
        compiler_params=params,
        cost_estimate=cost,
    )(place, rows, weight)


def enter_product(spot, slot, up, down, tok, place):
    out, scratch = split_parts(up.shape[1], spot.shape[0], slot.shape[1])
    return pl.pallas_call(
        enter_kernel,
        in_specs=[scalars, in_vmem, anywhere, anywhere, anywhere],
        out_specs=[anywhere, anywhere, in_vmem],
        out_shape=out + [jax.ShapeDtypeStruct((2 * tok, slot.shape[1]), bf16)],
        scratch_shapes=scratch
        + [
            pltpu.VMEM(held_shape(up, 0), bf16),
            pltpu.VMEM(held_shape(down, 1), bf16),
            pltpu.VMEM(slot.shape, bf16),
        ],
        compiler_params=params,
        cost_estimate=cost,
    )(place, spot, slot, up, down)


def rank_kernel(table_rows, place, row_ids, column_ids, spot, wanted, most):
    count, capacity = spot.shape[0], wanted.shape[0]
    shift = table_rows.bit_length() - 1
    across_ids, down_ids = row_ids[...], column_ids[...]
    here = lax.broadcasted_iota(jnp.int32, (count, count), 0)
    there = lax.broadcasted_iota(jnp.int32, (count, count), 1)
    equal = across_ids == down_ids
    same = (across_ids >> shift) == (down_ids >> shift)

    def ones(mask):
        return jnp.where(mask, 1.0, 0.0)

    repeat_down = jnp.sum(ones(equal & (there < here)), axis=1, keepdims=True)
    repeat_across = jnp.sum(ones(equal & (here < there)), axis=0, keepdims=True)
    number = jnp.sum(
        ones(same & (here < there) & (repeat_down == 0.0)), axis=0, keepdims=True
    )
    mine = jnp.sum(
        jnp.where(equal & (repeat_across == 0.0), number, 0.0), axis=1, keepdims=True
    )
    spot[...] = (down_ids >> shift) * capacity + mine.astype(jnp.int32)
    slot = lax.broadcasted_iota(jnp.int32, (capacity, count), 0)
    local = across_ids - (place[2] << shift)
    named = (
        (local >= 0)
        & (local < table_rows)
        & (repeat_across == 0.0)
        & (number.astype(jnp.int32) == slot)
    )
    wanted[...] = (
        jnp.sum(jnp.where(named, local.astype(f32) + 1.0, 0.0), axis=1, keepdims=True) - 1.0
    ).astype(jnp.int32)
    most[...] = jnp.max(mine, axis=0, keepdims=True).astype(jnp.int32) + 1


def rank(ids, table_rows, capacity, place):
    count = ids.shape[0]
    return pl.pallas_call(
        functools.partial(rank_kernel, table_rows),
        in_specs=[scalars, in_vmem, in_vmem],
        out_specs=[in_vmem] * 3,
        out_shape=[
            jax.ShapeDtypeStruct((count, 1), jnp.int32),
            jax.ShapeDtypeStruct((capacity, 1), jnp.int32),
            jax.ShapeDtypeStruct((1, 1), jnp.int32),
        ],
        compiler_params=params,
        cost_estimate=cost,
    )(place, ids[None, :], ids[:, None])


def join_kernel(dim, swapped, place, mine, other, weight, *refs):
    if swapped:
        instead, refs = refs[0], refs[1:]
    out, rows, staged, arrived, left, held = refs
    half = mine.shape[0]
    tiles = held.shape[0]

    def run():
        parts = [
            pltpu.make_async_copy(
                part,
                rows.at[pl.ds(pl.multiple_of(position * half, half), half)],
                arrived.at[tiles + index],
            )
            for index, (part, position) in enumerate(((mine, place[0]), (other, 1 - place[0])))
        ]
        for copy in parts:
            copy.start()
        copies = start_weight(weight, dim, held, arrived)
        for copy in parts:
            copy.wait()
        for index, copy in enumerate(copies):
            copy.wait()
            columns = slice(index * tile, (index + 1) * tile)
            staged[:, columns] = multiply(rows[...], held[index], dim).astype(bf16)
        done = pltpu.make_async_copy(staged, out, left.at[0])
        done.start()
        done.wait()

    if swapped:
        pl.when(place[1] == 0)(run)

        @pl.when(place[1] != 0)
        def _():
            copy = pltpu.make_async_copy(instead, out, left.at[0])
            copy.start()
            copy.wait()

    else:
        run()


def join_product(mine, other, weight, dim, place, instead=()):
    count = weight.shape[1 - dim]
    tiles = count // tile
    half, depth = mine.shape
    return pl.pallas_call(
        functools.partial(join_kernel, dim, bool(instead)),
        in_specs=[scalars] + [anywhere] * (3 + len(instead)),
        out_specs=anywhere,
        out_shape=jax.ShapeDtypeStruct((2 * half, count), bf16),
        scratch_shapes=[
            pltpu.VMEM((2 * half, depth), bf16),
            pltpu.VMEM((2 * half, count), bf16),
            pltpu.SemaphoreType.DMA((tiles + 2,)),
            pltpu.SemaphoreType.DMA((1,)),
            pltpu.VMEM(held_shape(weight, dim), bf16),
        ],
        compiler_params=params,
        cost_estimate=cost,
    )(place, mine, other, weight, *instead)


def lookup_kernel(wanted, table, out, chosen):
    @pl.when(pl.program_id(0) == 0)
    def _():
        row = lax.broadcasted_iota(jnp.int32, chosen.shape, 1)
        chosen[...] = jnp.where(row == wanted[...], 1.0, 0.0).astype(bf16)

    out[...] = multiply(chosen[...], table[...], 0).astype(bf16)


def lookup(wanted, table):
    count = wanted.shape[0]
    rows, feat = table.shape
    return pl.pallas_call(
        lookup_kernel,
        grid=(feat // tile,),
        in_specs=[
            pl.BlockSpec(wanted.shape, lambda i: (0, 0)),
            pl.BlockSpec((rows, tile), lambda i: (0, i)),
        ],
        out_specs=pl.BlockSpec((count, tile), lambda i: (0, i)),
        scratch_shapes=[pltpu.VMEM((count, rows), bf16)],
        out_shape=jax.ShapeDtypeStruct((count, feat), bf16),
        compiler_params=params,
        cost_estimate=cost,
    )(wanted, table)


def tie(*values):
    return lax.optimization_barrier(values)


def after(value, *earlier):
    return lax.optimization_barrier((value, *earlier))[0]


def on_device(token_ids, table, w_up, w_down, cotangent):
    micro, tok, feat = cotangent.shape
    dp = lax.axis_size("dp")
    up = w_up[0]
    down = w_down[0]
    is_first = lax.axis_index("segment") == 0
    here = lax.axis_index("dp")
    place = jnp.stack(
        [lax.axis_index("mp") % 2, lax.axis_index("segment"), here]
    ).astype(jnp.int32)
    capacity = micro * tok
    table_rows = table.shape[0]
    own_cot = cotangent.reshape(capacity, feat)

    def whole(slot):
        return slot.reshape(-1, feat)

    def blocks(rows):
        return rows.reshape(dp, -1, feat)

    def either(left, right):
        return jnp.where(is_first, left, right)

    def chip_sum(kept, sent):
        return (kept.astype(f32) + swap(sent, 1).astype(f32)).astype(bf16)

    def finish(chip, came):
        return chip.astype(f32) + came.astype(f32)

    def active(summed):
        return gelu_value(summed.astype(f32)).astype(bf16)

    def slope(saved, summed):
        return (gelu_slope(saved) * summed.astype(f32)).astype(bf16)

    spot, wanted, most = rank(token_ids.reshape(-1), table_rows, capacity, place)
    fits = most[0, 0] <= capacity

    def sparse():
        return lookup(wanted, table)

    def dense():
        by_owner = token_ids.reshape(micro, dp, tok).transpose(1, 0, 2).reshape(-1, 1)
        fetched = lookup(by_owner - here * table_rows, table)
        return collect(exchange(blocks(fetched))).astype(bf16)

    found = lax.cond(fits, sparse, dense)
    slot_2 = whole(exchange(spread(either(found, own_cot))))
    token = jnp.arange(micro * dp * tok, dtype=jnp.int32)
    in_order = (token // tok % dp) * capacity + token // (dp * tok) * tok + token % tok
    spot = jnp.where(is_first & fits, spot, in_order[:, None])
    spot = spot.reshape(micro, 2, -1).transpose(1, 0, 2).reshape(-1, 1)

    kept, sent, embedded = enter_product(spot, slot_2, up, down, tok, place)
    chip = chip_sum(kept, sent)
    half = chip.shape[0] // 2
    emb_a, emb_b = embedded[:tok], embedded[tok:]
    came_a, came_b = swap(chip[:half], 2), swap(chip[half:], 2)
    first_a = finish(chip[:half], came_a)
    hid_a, first_a = active(first_a), first_a.astype(bf16)
    mix_a = join_product(hid_a, swap(hid_a, 1), down, 0, place)
    slot_4 = exchange(blocks(mix_a))
    first_b = finish(chip[half:], after(came_b, mix_a))
    hid_b, first_b = active(first_b), first_b.astype(bf16)
    mix_b = join_product(hid_b, swap(hid_b, 1), down, 0, place)
    act0_a = plus(emb_a, after(slot_4, mix_b))
    pass_a = across(act0_a)

    slot_5 = exchange(after(either(blocks(mix_b), spread(pass_a)), slot_4))
    slope_a = gelu_slope(after(first_a, mix_b).astype(f32)).astype(bf16)
    slope_b = gelu_slope(after(first_b, mix_b).astype(f32)).astype(bf16)
    slot_5 = after(slot_5, slope_a, slope_b)
    act0_b = plus(emb_b, slot_5)
    pass_b = across(act0_b)
    kept_a, sent_a = split_product(whole(after(slot_5, act0_b)), up, 0, place)
    pass_b, kept_a, sent_a = tie(pass_b, kept_a, sent_a)
    chip_a = chip_sum(kept_a, sent_a)
    came_a = swap(chip_a, 2)
    slot_6 = exchange(after(spread(after(pass_b, kept_a)), slot_5))
    pre_a = finish(chip_a, came_a)
    back_a = slope(pre_a, first_a)
    pre_a = pre_a.astype(bf16)
    mix_a = join_product(back_a, swap(back_a, 1), up, 1, place)
    kept_b, sent_b = split_product(whole(after(slot_6, mix_a)), up, 0, place)
    slot_7 = exchange(after(blocks(mix_a), slot_6))
    chip_b = chip_sum(kept_b, sent_b)
    came_b = swap(chip_b, 2)
    hid_a = active(after(pre_a, chip_b))
    out_a = join_product(hid_a, swap(hid_a, 1), down, 0, place)
    grad1_a = plus(cotangent[0], after(slot_7, out_a))
    gone_a = across(grad1_a)
    pre_b = finish(chip_b, after(came_b, grad1_a))
    back_b = slope(pre_b, first_b)
    pre_b = pre_b.astype(bf16)
    mix_b = join_product(back_b, swap(back_b, 1), up, 1, place)
    slot_8 = exchange(
        after(either(spread(after(gone_a, mix_b)), blocks(mix_b)), slot_7)
    )
    hid_b = active(after(pre_b, mix_b))
    out_b = join_product(hid_b, swap(hid_b, 1), down, 0, place)
    slot_8 = after(slot_8, out_b)

    grad1_b = plus(cotangent[1], slot_8)
    gone_b = across(grad1_b)
    kept_a, sent_a = split_product(whole(after(slot_8, grad1_b)), down, 1, place)
    send_9 = either(spread(gone_b), blocks(out_a))
    send_9, kept_a, sent_a = tie(send_9, kept_a, sent_a)
    slot_9 = exchange(after(send_9, slot_8))
    chip_a = chip_sum(kept_a, sent_a)
    came_a = swap(chip_a, 2)
    kept_b, sent_b = split_product(whole(slot_9), down, 1, place)
    back_a = (slope_a.astype(f32) * finish(chip_a, after(came_a, kept_b))).astype(bf16)
    far_a = swap(back_a, 1)
    chip_b = chip_sum(kept_b, sent_b)
    came_b = swap(chip_b, 2)
    mix_a = join_product(after(back_a, chip_b), far_a, up, 1, place, (out_b,))
    slot_10 = exchange(after(blocks(mix_a), slot_9))
    act1_a = plus(pass_a, after(slot_9, mix_a))
    back_b = (slope_b.astype(f32) * finish(chip_b, after(came_b, act1_a))).astype(bf16)
    mix_b = join_product(back_b, swap(back_b, 1), up, 1, place)
    slot_11 = exchange(after(blocks(mix_b), slot_10))
    act1_b = plus(pass_b, slot_10)
    grad0_a = plus(gone_a, slot_10)
    grad0_b = plus(gone_b, after(slot_11, act1_b, grad0_a))

    acts = jnp.stack([either(act0_a, act1_a), either(act0_b, act1_b)])
    grads = jnp.stack([either(grad0_a, grad1_a), either(grad0_b, grad1_b)])
    return (acts[None], grads[None])


def solution(mesh):
    return jax.shard_map(
        on_device,
        mesh=mesh,
        in_specs=(
            P(),
            P("dp", "mp"),
            P("segment", "mp", "dp"),
            P("segment", "dp", "mp"),
            P(None, "dp", "mp"),
        ),
        out_specs=(P("segment", None, "dp", "mp"), P("segment", None, "dp", "mp")),
        check_vma=False,
    )
```
